32 devices in a mesh: neur: 2 (over x), tm: 16 (over z, y, core).
Axes of the slice: x: 2, y: 2, z: 4, core: 2. Of those that a mesh axis runs over, the one named last changes fastest.
Arguments:
- counts: float32 [512, 8192], P('neur', 'tm'), may hold values from 200 to 10000
- motifs: float32 [512, 8, 128], P('neur'), may hold values from 0.2 to 5
- loadings: float32 [8, 8192], P(None, 'tm'), may hold values from 0.2 to 5
Outputs:
- new_motifs: float32 [512, 8, 128], P('neur')
- new_loadings: float32 [8, 8192], P(None, 'tm')
The draws below stay inside these ranges and needn't reach their ends.
All inputs are finite; a program needn't handle non-finite values.
Results may differ from the reference program's by a relative error of at most 0.000071.
Values sent between devices are 32-bit elements; how exact they have to be, the bound alone decides.
No kernel may reach another device: no remote copies, remote signals or barrier semaphores. Data moves between devices by JAX's collectives and lax.ppermute only.
A program may use at most 64 MiB of HBM per device.

```python
import math
import jax
import jax.numpy as jnp
from jax import lax

K = 8
L = 128
NEUR = 512
FRAMES = 8192


def block_scale(own_key, shape, split, low, top_value):
    level = 1.0
    for axis_at, shards_of in split:
        steps = jax.random.uniform(jax.random.fold_in(jax.random.fold_in(own_key, 6), axis_at), (shards_of,), jnp.float32, low / len(split), top_value / len(split))
        level = level * jnp.repeat(jnp.exp(steps), shape[axis_at] // shards_of).reshape((-1,) + (1,) * (len(shape) - 1 - axis_at))
    return level


def setup_inputs(seed: int = 0) -> dict:
    seeds = jax.random.split(jax.random.key(seed), 4)
    return {
        "counts": jnp.clip(jnp.exp(math.log(10000.0) - 3.912023 * jax.random.uniform(seeds[0], (NEUR, FRAMES), jnp.float32) ** block_scale(seeds[0], (NEUR, FRAMES), ((0, 2), (1, 16)), -0.2, 0.2)), 200.0, 10000.0),
        "motifs": jnp.clip(jnp.exp(math.log(5.0) - 3.218876 * jax.random.uniform(seeds[1], (NEUR, K, L), jnp.float32) ** block_scale(seeds[1], (NEUR, K, L), ((0, 2),), -0.2, 0.2)), 0.2, 5.0),
        "loadings": jnp.clip(jnp.exp(math.log(5.0) - 3.218876 * jax.random.uniform(seeds[2], (K, FRAMES), jnp.float32) ** block_scale(seeds[2], (K, FRAMES), ((1, 16),), -0.2, 0.2)), 0.2, 5.0),
    }


def skew_left(field, out_width):
    batch_size, lag_count, span_len = field.shape
    flat_rows = field.reshape(batch_size, lag_count * span_len)
    flat_rows = jnp.pad(flat_rows, ((0, 0), (0, lag_count)))
    return flat_rows.reshape(batch_size, lag_count, span_len + 1)[:, :, :out_width]


def toeplitz(extended, lag_count, out_width):
    stacked = jnp.broadcast_to(extended[:, None, :], (extended.shape[0], lag_count, extended.shape[1]))
    return skew_left(stacked, out_width)[:, ::-1, :]


def reference(counts, motifs, loadings):
    highest = lax.Precision.HIGHEST
    padded_loadings = jnp.pad(loadings, ((0, 0), (L - 1, 0)))
    shifted = toeplitz(padded_loadings, L, FRAMES).reshape(K * L, FRAMES)
    motif_mat = motifs.reshape(NEUR, K * L)
    estimate = jnp.dot(motif_mat, shifted, precision=highest)
    ratio_field = counts / estimate
    numer_w = lax.dot_general(ratio_field, shifted, (((1,), (1,)), ((), ())), precision=highest)
    denom_w = jnp.sum(shifted, axis=1).reshape(K, L)
    new_motifs = motifs * numer_w.reshape(NEUR, K, L) / denom_w
    ratio_ext = jnp.pad(ratio_field, ((0, 0), (0, L - 1)))
    lagged = lax.dot_general(motif_mat, ratio_ext, (((0,), (0,)), ((), ())), precision=highest)
    numer_h = jnp.sum(skew_left(lagged.reshape(K, L, FRAMES + L - 1), FRAMES), axis=1)
    motif_tot = jnp.sum(motifs, axis=0)
    lag_index = jnp.arange(L, dtype=jnp.int32)[:, None]
    frame_index = jnp.arange(FRAMES, dtype=jnp.int32)[None, :]
    valid = (lag_index + frame_index < FRAMES).astype(jnp.float32)
    denom_h = jnp.dot(motif_tot, valid, precision=highest)
    new_loadings = loadings * numer_h / denom_h
    return new_motifs, new_loadings
```

```python
import jax
import jax.numpy as jnp
from jax import lax
from jax.experimental import pallas as pl
from jax.experimental.pallas import tpu as pltpu
from jax.sharding import PartitionSpec as P

F32, BF16 = jnp.float32, jnp.bfloat16
NN = (((1,), (0,)), ((), ()))
NT = (((1,), (1,)), ((), ()))
TN = (((0,), (0,)), ((), ()))
VMEM_LIMIT = 24 * 1024 * 1024


def split(x):
    high = x.astype(BF16)
    return high, (x - high.astype(F32)).astype(BF16)


def dot3(ah, al, bh, bl, dims):
    def dot(a, b):
        return lax.dot_general(a, b, dims, preferred_element_type=F32)

    return dot(ah, bh) + (dot(ah, bl) + dot(al, bh))


def toeplitz(row, lags):
    return pltpu.roll(jnp.broadcast_to(row, (lags, row.shape[1])), 0, 1, stride=1, stride_axis=0)


def vmem_call(kernel, out_shapes, scalars=0, name=None, flops=0):
    def call(*args):
        specs = [pl.BlockSpec(memory_space=pltpu.SMEM)] * scalars
        specs += [pl.BlockSpec(memory_space=pltpu.VMEM)] * (len(args) - scalars)
        moved = sum(a.size * a.dtype.itemsize for a in args)
        return pl.pallas_call(
            kernel,
            out_shape=out_shapes,
            in_specs=specs,
            out_specs=[pl.BlockSpec(memory_space=pltpu.VMEM)] * len(out_shapes),
            compiler_params=pltpu.CompilerParams(vmem_limit_bytes=VMEM_LIMIT),
            cost_estimate=pl.CostEstimate(flops=flops, bytes_accessed=moved, transcendentals=0),
            name=name,
        )(*args)

    return call


def body_kernel(counts_ref, motifs_ref, loads_ref, mh_ref, ml_ref, th_ref, tl_ref, rh_ref, rl_ref):
    rows = counts_ref.shape[0]
    motif_count = loads_ref.shape[0]
    lags = motifs_ref.shape[1]
    for k in range(motif_count):
        at = pl.ds(k * lags, lags)
        mh_ref[:, at], ml_ref[:, at] = split(motifs_ref[pl.ds(k, rows, stride=motif_count), :])
        th_ref[at, :], tl_ref[at, :] = split(toeplitz(loads_ref[pl.ds(k, 1), :], lags)[:, lags:])
    estimate = dot3(mh_ref[...], ml_ref[...], th_ref[...], tl_ref[...], NN)
    rh_ref[...], rl_ref[...] = split(counts_ref[:, lags:] / estimate)


def head_kernel(core_ref, tail_ref, counts_ref, loads_ref, mh_ref, ml_ref, th_ref, tl_ref, rh_ref, rl_ref,
                send_ref, keep_ref, fh_ref, fl_ref, hh, hl):
    rows = counts_ref.shape[0]
    motif_count = loads_ref.shape[0]
    lags = mh_ref.shape[1] // motif_count
    half = rows // 2
    frames = loads_ref.shape[1]
    for k in range(motif_count):
        at = pl.ds(k * lags, lags)
        row = jnp.concatenate([tail_ref[pl.ds(k, 1), frames - lags:], loads_ref[pl.ds(k, 1), :lags]], axis=1)
        hh[at, :], hl[at, :] = split(toeplitz(row, lags)[:, lags:])
    estimate = dot3(mh_ref[...], ml_ref[...], hh[...], hl[...], NN)
    head_h, head_l = split(counts_ref[:, :lags] / estimate)
    fh_ref[:, :lags], fl_ref[:, :lags] = head_h, head_l
    fh_ref[:, lags:], fl_ref[:, lags:] = rh_ref[...], rl_ref[...]
    core = core_ref[0]
    away, home = pl.ds(pl.multiple_of((1 - core) * half, half), half), pl.ds(pl.multiple_of(core * half, half), half)
    ones = jnp.ones((16, frames), BF16)
    xh = jnp.concatenate([fh_ref[away, :], fh_ref[home, :], ones], axis=0)
    xl = jnp.concatenate([fl_ref[away, :], fl_ref[home, :], jnp.zeros_like(ones)], axis=0)
    for k in range(motif_count):
        at = pl.ds(k * lags, lags)
        kh = jnp.concatenate([hh[at, :], th_ref[at, :]], axis=1)
        kl = jnp.concatenate([hl[at, :], tl_ref[at, :]], axis=1)
        numer = dot3(xh, xl, kh, kl, NT)
        send_ref[pl.ds(k, half, stride=motif_count), :] = numer[:half]
        keep_ref[pl.ds(k, half, stride=motif_count), :] = numer[half:rows]
        send_ref[pl.ds(half * motif_count + k, 1), :] = numer[rows:rows + 1]
        keep_ref[pl.ds(half * motif_count + k, 1), :] = numer[rows:rows + 1]


def fold_kernel(bit_ref, mine_ref, got_ref, send_ref, keep_ref):
    half = (mine_ref.shape[0] - 1) // 2
    bit = bit_ref[0]
    for out, place in ((send_ref, 1 - bit), (keep_ref, bit)):
        at = pl.ds(place * half, half)
        out[:half] = mine_ref[at] + got_ref[at]
        out[half:] = mine_ref[2 * half:] + got_ref[2 * half:]


def update_kernel(at_ref, mine_ref, got_ref, motifs_ref, out_ref):
    rows = out_ref.shape[0]
    denom = mine_ref[rows] + got_ref[rows]
    numer = mine_ref[:rows] + got_ref[:rows]
    out_ref[...] = motifs_ref[pl.ds(at_ref[0], rows)] * numer / denom[None]


def join_kernel(bit_ref, mine_ref, got_ref, out_ref):
    half = mine_ref.shape[0]
    bit = bit_ref[0]
    out_ref[pl.ds(bit * half, half)] = mine_ref[...]
    out_ref[pl.ds((1 - bit) * half, half)] = got_ref[...]


def lagged_kernel(mh_ref, ml_ref, fh_ref, fl_ref, motifs_ref, numer_ref, ahead_ref, total_ref):
    motif_count, frames = numer_ref.shape
    lags = mh_ref.shape[1] // motif_count
    width = frames + lags
    down = lax.broadcasted_iota(jnp.int32, (lags, lags), 0)
    across = lax.broadcasted_iota(jnp.int32, (lags, lags), 1)
    flip = (down + across == lags - 1).astype(BF16)
    for k in range(motif_count):
        at = pl.ds(k * lags, lags)
        ph, pw = (
            lax.dot_general(ref[:, at], flip, NN, preferred_element_type=F32).astype(BF16) for ref in (mh_ref, ml_ref)
        )
        lagged = dot3(ph, pw, fh_ref[...], fl_ref[...], TN)
        wide = jnp.concatenate([jnp.zeros((lags, lags), F32), lagged], axis=1)
        skewed = pltpu.roll(wide, width - (lags - 1), 1, stride=1, stride_axis=0)
        numer = jnp.sum(skewed, axis=0, keepdims=True)
        ahead_ref[pl.ds(k, 1), :] = numer[:, :lags]
        numer_ref[pl.ds(k, 1), :] = numer[:, lags:]
    total_ref[...] = jnp.sum(motifs_ref[...], axis=0)


def halo_kernel(numer_ref, ahead_ref, total_ref, out_ref):
    frames, lags = numer_ref.shape[1], ahead_ref.shape[1]
    out_ref[:, :frames - lags] = numer_ref[:, :frames - lags]
    out_ref[:, frames - lags:frames] = numer_ref[:, frames - lags:] + ahead_ref[...]
    out_ref[:, frames:] = total_ref[...]


def pair_kernel(mine_ref, got_ref, out_ref):
    out_ref[...] = mine_ref[...] + got_ref[...]


def loads_kernel(left_ref, mine_ref, got_ref, loads_ref, out_ref):
    frames = loads_ref.shape[1]
    lags = mine_ref.shape[1] - frames
    both = mine_ref[...] + got_ref[...]
    lag = lax.broadcasted_iota(jnp.int32, (lags, frames), 0)
    frame = lax.broadcasted_iota(jnp.int32, (lags, frames), 1)
    valid = (lag + frame < left_ref[0]).astype(F32)
    denom = lax.dot_general(both[:, frames:], valid, NN, precision=lax.Precision.HIGHEST, preferred_element_type=F32)
    out_ref[...] = loads_ref[...] * both[:, :frames] / denom


def body(counts, motifs, loadings):
    rows, motif_count, lags = motifs.shape
    frames = loadings.shape[1]
    ranks, me = lax.axis_size("tm"), lax.axis_index("tm")
    steps = ranks.bit_length() - 1
    assert ranks == 1 << steps and steps >= 3 and rows % ranks == 0

    def shape(*dims, dtype=F32):
        return jax.ShapeDtypeStruct(dims, dtype)

    orders = [[0, 1, 2, *range(3, steps)], [0, 2, 1, *range(3, steps)]]
    core = me & 1

    def bit(step):
        return jnp.where(core == 0, (me >> orders[0][step]) & 1, (me >> orders[1][step]) & 1).astype(jnp.int32)

    def swap(x, step):
        return lax.ppermute(x, "tm", [(i, i ^ (1 << orders[i & 1][step])) for i in range(ranks)])

    tail = lax.ppermute(loadings, "tm", [(i, i + 1) for i in range(ranks - 1)])
    flat = motifs.reshape(rows * motif_count, lags)
    depth = motif_count * lags
    macs = rows * depth * frames * 6
    mh, ml, th, tl, rh, rl = vmem_call(
        body_kernel,
        [shape(rows, depth, dtype=BF16)] * 2 + [shape(depth, frames - lags, dtype=BF16)] * 2
        + [shape(rows, frames - lags, dtype=BF16)] * 2,
        name="body", flops=macs,
    )(counts, flat, loadings)
    half = rows // 2
    send, keep, fh, fl = pl.pallas_call(
        head_kernel,
        out_shape=[shape((half + 1) * motif_count, lags)] * 2 + [shape(rows, frames, dtype=BF16)] * 2,
        in_specs=[pl.BlockSpec(memory_space=pltpu.SMEM)] + [pl.BlockSpec(memory_space=pltpu.VMEM)] * 9,
        out_specs=[pl.BlockSpec(memory_space=pltpu.VMEM)] * 4,
        scratch_shapes=[pltpu.VMEM((depth, lags), BF16)] * 2,
        compiler_params=pltpu.CompilerParams(vmem_limit_bytes=VMEM_LIMIT),
        name="head",
    )(core.reshape(1), tail, counts, loadings, mh, ml, th, tl, rh, rl)
    send = send.reshape(half + 1, motif_count, lags)
    keep = keep.reshape(half + 1, motif_count, lags)

    numer, ahead, total = vmem_call(
        lagged_kernel, [shape(motif_count, frames), shape(motif_count, lags), shape(motif_count, lags)],
        name="lagged", flops=macs,
    )(mh, ml, fh, fl, motifs)
    ahead = lax.ppermute(ahead, "tm", [(i, i - 1) for i in range(1, ranks)])
    (loads_part,) = vmem_call(halo_kernel, [shape(motif_count, frames + lags)], name="halo")(numer, ahead, total)

    own = bit(0) * half
    got = swap(send, 0)
    for step in range(1, steps - 1):
        half //= 2
        here = bit(step)
        send, keep = vmem_call(fold_kernel, [shape(half + 1, motif_count, lags)] * 2, 1, name="fold")(
            here.reshape(1), keep, got
        )
        own = own + here * half
        got = swap(send, step)
    (keep,) = vmem_call(pair_kernel, [shape(half + 1, motif_count, lags)], name="pair")(keep, got)
    got = swap(keep, steps - 1)
    (mine,) = vmem_call(update_kernel, [shape(half, motif_count, lags)], 1, name="update")(
        own.reshape(1), keep, got, motifs
    )
    for step in range(steps - 2, -1, -1):
        got = swap(mine, step)
        half *= 2
        (mine,) = vmem_call(join_kernel, [shape(half, motif_count, lags)], 1, name="join")(
            bit(step).reshape(1), mine, got
        )

    groups = lax.axis_size("neur")
    flips = groups.bit_length() - 1
    assert groups == 1 << flips
    for flip in range(flips):
        got = lax.ppermute(loads_part, "neur", [(i, i ^ (1 << flip)) for i in range(groups)])
        if flip < flips - 1:
            (loads_part,) = vmem_call(pair_kernel, [loads_part], name="pair")(loads_part, got)
    if flips == 0:
        got = jnp.zeros_like(loads_part)
    left = (ranks - me) * frames
    (new_loadings,) = vmem_call(loads_kernel, [shape(motif_count, frames)], 1, name="loads")(
        left.astype(jnp.int32).reshape(1), loads_part, got, loadings
    )
    return mine, new_loadings


def solution(mesh):
    in_specs = (P("neur", "tm"), P("neur", None, None), P(None, "tm"))
    out_specs = (P("neur", None, None), P(None, "tm"))
    return jax.shard_map(body, mesh=mesh, in_specs=in_specs, out_specs=out_specs, check_vma=False)
```

```python
import functools

import jax
import jax.numpy as jnp
from jax import lax
from jax.experimental import pallas as pl
from jax.experimental.pallas import tpu as pltpu
from jax.sharding import PartitionSpec as P

F32, BF16 = jnp.float32, jnp.bfloat16
NN = (((1,), (0,)), ((), ()))
NT = (((1,), (1,)), ((), ()))
TN = (((0,), (0,)), ((), ()))
MIB = 1024 * 1024
BODY_LIMIT = 20
ONES = 16
CHUNKS = 2


def split(x):
    high = x.astype(BF16)
    return high, (x - high.astype(F32)).astype(BF16)


def dot3(ah, al, bh, bl, dims):
    def dot(a, b):
        return lax.dot_general(a, b, dims, preferred_element_type=F32)

    return dot(ah, bh) + (dot(ah, bl) + dot(al, bh))


def toeplitz(row, lags):
    return pltpu.roll(jnp.broadcast_to(row, (lags, row.shape[1])), 0, 1, stride=1, stride_axis=0)


def place(me, step, steps):
    first, second = (order(core, steps)[step] for core in range(2))
    return jnp.where(me & 1 == 0, (me >> first) & 1, (me >> second) & 1)


def order(core, steps):
    return [0, 2, 1, *range(3, steps)] if core else list(range(steps))


def call(kernel, out_shapes, *args, limit=4, spaces=None, outs=None, scratch=(), aliases=None, flops=0, moved=0):
    spaces = spaces or [pltpu.VMEM] * (len(args) - 1)
    outs = outs or [pltpu.VMEM] * len(out_shapes)
    return pl.pallas_call(
        kernel,
        out_shape=out_shapes,
        in_specs=[pl.BlockSpec(memory_space=space) for space in [pltpu.SMEM, *spaces]],
        out_specs=[pl.BlockSpec(memory_space=space) for space in outs],
        scratch_shapes=list(scratch),
        input_output_aliases=aliases or {},
        compiler_params=pltpu.CompilerParams(vmem_limit_bytes=int(limit * MIB)),
        cost_estimate=pl.CostEstimate(flops=flops, bytes_accessed=moved, transcendentals=0),
        name=getattr(kernel, "func", kernel).__name__,
    )(*args)


def body_kernel(me_ref, counts_hbm, motifs_hbm, loads_hbm, mh_ref, ml_ref, rh_ref, rl_ref, numer_ref, counts_ref,
                loads_ref, total_ref, motifs_ref, rest_ref, th, tl, sems):
    rows, frames = counts_hbm.shape
    motif_count = loads_ref.shape[0]
    lags = counts_ref.shape[1]
    copies = [
        pltpu.make_async_copy(loads_hbm, loads_ref, sems.at[0]),
        pltpu.make_async_copy(motifs_hbm, motifs_ref, sems.at[1]),
        pltpu.make_async_copy(counts_hbm.at[:, pl.ds(lags, frames - lags)], rest_ref, sems.at[2]),
        pltpu.make_async_copy(counts_hbm.at[:, pl.ds(0, lags)], counts_ref, sems.at[3]),
    ]
    for copy in copies:
        copy.start()
    copies[0].wait()
    for k in range(motif_count):
        at = pl.ds(k * lags, lags)
        th[at, :], tl[at, :] = split(toeplitz(loads_ref[pl.ds(k, 1), :], lags)[:, lags:])
    copies[1].wait()
    for k in range(motif_count):
        at = pl.ds(k * lags, lags)
        mh_ref[:, at], ml_ref[:, at] = split(motifs_ref[pl.ds(k, rows, stride=motif_count), :])
    estimate = dot3(mh_ref[...], ml_ref[...], th[...], tl[...], NN)
    copies[2].wait()
    rh_ref[...], rl_ref[...] = split(rest_ref[...] / estimate)
    ones = jnp.ones((ONES, frames - lags), BF16)
    xh = jnp.concatenate([rh_ref[...], ones], axis=0)
    xl = jnp.concatenate([rl_ref[...], jnp.zeros_like(ones)], axis=0)
    for k in range(0, motif_count, 2):
        at = pl.ds(k * lags, 2 * lags)
        numer_ref[:, at] = dot3(xh, xl, th[at, :], tl[at, :], NT)
    total_ref[...] = jnp.sum(motifs_ref[...].reshape(rows, motif_count, lags), axis=0)
    copies[3].wait()


def numer_rows(numer, motif_count, out_ref, count):
    lags = out_ref.shape[-1]
    for k in range(motif_count):
        out_ref[pl.ds(k, count, stride=motif_count), :] = numer[:count, k * lags:(k + 1) * lags]


def head_kernel(chunks, me_ref, tail_ref, counts_ref, loads_ref, mh_ref, ml_ref, numer_ref, *refs):
    *send_refs, fh_ref, fl_ref, hh_ref, hl_ref, denom_ref = refs
    rows, lags = counts_ref.shape
    motif_count, frames = loads_ref.shape
    for k in range(motif_count):
        at = pl.ds(k * lags, lags)
        row = jnp.concatenate([tail_ref[pl.ds(k, 1), frames - lags:], loads_ref[pl.ds(k, 1), :lags]], axis=1)
        hh_ref[at, :], hl_ref[at, :] = split(toeplitz(row, lags)[:, lags:])
    estimate = dot3(mh_ref[...], ml_ref[...], hh_ref[...], hl_ref[...], NN)
    fh_ref[...], fl_ref[...] = split(counts_ref[...] / estimate)
    half = rows // chunks // 2
    away = [pl.ds(pl.multiple_of((2 * c + 1 - (me_ref[0] & 1)) * half, half), half) for c in range(chunks)]
    ones = jnp.ones((ONES, lags), BF16)
    xh = jnp.concatenate([*(fh_ref[at, :] for at in away), ones], axis=0)
    xl = jnp.concatenate([*(fl_ref[at, :] for at in away), jnp.zeros_like(ones)], axis=0)
    for k in range(0, motif_count, 2):
        at = pl.ds(k * lags, 2 * lags)
        numer = dot3(xh, xl, hh_ref[at, :], hl_ref[at, :], NT)
        for j in range(2):
            there, here = pl.ds((k + j) * lags, lags), slice(j * lags, (j + 1) * lags)
            for c in range(chunks):
                send_refs[c][pl.ds(k + j, half, stride=motif_count), :] = (
                    numer[c * half:(c + 1) * half, here] + numer_ref[away[c], there]
                )
            denom = numer[chunks * half:chunks * half + 1, here] + numer_ref[pl.ds(rows, 1), there]
            send_refs[0][pl.ds(half * motif_count + k + j, 1), :] = denom
            denom_ref[pl.ds(k + j, 1), :] = denom


def home_kernel(chunks, me_ref, fh_ref, fl_ref, hh_ref, hl_ref, denom_ref, numer_ref, *keep_refs):
    rows, lags = fh_ref.shape
    motif_count = denom_ref.shape[0]
    half = rows // chunks // 2
    home = [pl.ds(pl.multiple_of((2 * c + (me_ref[0] & 1)) * half, half), half) for c in range(chunks)]
    xh = jnp.concatenate([fh_ref[at, :] for at in home], axis=0)
    xl = jnp.concatenate([fl_ref[at, :] for at in home], axis=0)
    for k in range(0, motif_count, 2):
        at = pl.ds(k * lags, 2 * lags)
        numer = dot3(xh, xl, hh_ref[at, :], hl_ref[at, :], NT)
        for j in range(2):
            there, here = pl.ds((k + j) * lags, lags), slice(j * lags, (j + 1) * lags)
            for c in range(chunks):
                keep_refs[c][pl.ds(k + j, half, stride=motif_count), :] = (
                    numer[c * half:(c + 1) * half, here] + numer_ref[home[c], there]
                )
    keep_refs[0][pl.ds(half * motif_count, motif_count), :] = denom_ref[...]


def fold_kernel(step, steps, half, me_ref, mine_ref, got_ref, send_ref, keep_ref):
    bit = place(me_ref[0], step, steps)
    for out, part in ((send_ref, 1 - bit), (keep_ref, bit)):
        at = pl.ds(part * half, half)
        out[:half] = mine_ref[at] + got_ref[at]
        if out.shape[0] > half:
            out[half:] = mine_ref[2 * half:] + got_ref[2 * half:]


def pair_kernel(me_ref, mine_ref, got_ref, out_ref):
    out_ref[...] = mine_ref[...] + got_ref[...]


def update_kernel(chunk, steps, me_ref, mine_ref, got_ref, denom_ref, motifs_ref, out_ref, *denom_out):
    rows = out_ref.shape[0]
    at, size = chunk, rows << (steps - 1)
    at = chunk * size
    for step in range(steps - 1):
        size //= 2
        at = at + place(me_ref[0], step, steps) * size
    numer = mine_ref[:rows] + got_ref[:rows]
    if denom_out:
        denom = mine_ref[rows] + got_ref[rows]
        denom_out[0][...] = denom
    else:
        denom = denom_ref[...]
    out_ref[...] = motifs_ref[pl.ds(at, rows)] * numer / denom[None]


def join_kernel(step, steps, me_ref, mine_ref, got_ref, out_ref):
    half = mine_ref.shape[0]
    bit = place(me_ref[0], step, steps)
    out_ref[pl.ds(bit * half, half)] = mine_ref[...]
    out_ref[pl.ds((1 - bit) * half, half)] = got_ref[...]


def store_kernel(parts, me_ref, *refs):
    blocks, out_hbm, sems = refs[:len(parts)], refs[-2], refs[-1]
    core = me_ref[0] & 1
    copies = []
    for i, ((at, own), block) in enumerate(zip(parts, blocks)):
        rows = block.shape[0]
        at = at + (core if own else 1 - core) * rows
        copies.append(pltpu.make_async_copy(block, out_hbm.at[pl.ds(at, rows)], sems.at[i]))
    for copy in copies:
        copy.start()
    for copy in copies:
        copy.wait()


def lagged_kernel(me_ref, mh_ref, ml_ref, fh_ref, fl_ref, rh_ref, rl_ref, numer_ref, ahead_ref, ph, pw):
    motif_count, frames = numer_ref.shape
    lags = ahead_ref.shape[1]
    width = frames + lags
    down = lax.broadcasted_iota(jnp.int32, (lags, lags), 0)
    across = lax.broadcasted_iota(jnp.int32, (lags, lags), 1)
    flip = (down + across == lags - 1).astype(BF16)
    xh = jnp.concatenate([fh_ref[...], rh_ref[...]], axis=1)
    xl = jnp.concatenate([fl_ref[...], rl_ref[...]], axis=1)
    for k in range(motif_count):
        at = pl.ds(k * lags, lags)
        for ref, out in ((mh_ref, ph), (ml_ref, pw)):
            out[:, at] = lax.dot_general(ref[:, at], flip, NN, preferred_element_type=F32).astype(BF16)
    for k in range(0, motif_count, 4):
        at = pl.ds(k * lags, 4 * lags)
        lagged = dot3(ph[:, at], pw[:, at], xh, xl, TN)
        for j in range(4):
            wide = jnp.concatenate([jnp.zeros((lags, lags), F32), lagged[j * lags:(j + 1) * lags]], axis=1)
            skewed = pltpu.roll(wide, width - (lags - 1), 1, stride=1, stride_axis=0)
            numer = jnp.sum(skewed, axis=0, keepdims=True)
            ahead_ref[pl.ds(k + j, 1), :] = numer[:, :lags]
            numer_ref[pl.ds(k + j, 1), :] = numer[:, lags:]


def halo_kernel(me_ref, numer_ref, ahead_ref, total_ref, out_ref):
    frames, lags = numer_ref.shape[1], ahead_ref.shape[1]
    out_ref[:, :frames - lags] = numer_ref[:, :frames - lags]
    out_ref[:, frames - lags:frames] = numer_ref[:, frames - lags:] + ahead_ref[...]
    out_ref[:, frames:] = total_ref[...]


def loads_kernel(ranks, me_ref, mine_ref, got_ref, loads_ref, out_ref):
    frames = loads_ref.shape[1]
    lags = mine_ref.shape[1] - frames
    both = mine_ref[...] + got_ref[...]
    left = (ranks - me_ref[0]) * frames
    lag = lax.broadcasted_iota(jnp.int32, (lags, frames), 0)
    frame = lax.broadcasted_iota(jnp.int32, (lags, frames), 1)
    valid = (lag + frame < left).astype(F32)
    denom = lax.dot_general(both[:, frames:], valid, NN, precision=lax.Precision.HIGHEST, preferred_element_type=F32)
    out_ref[...] = loads_ref[...] * both[:, :frames] / denom


def body(counts, motifs, loadings):
    rows, motif_count, lags = motifs.shape
    frames = loadings.shape[1]
    ranks, groups = lax.axis_size("tm"), lax.axis_size("neur")
    steps, flips = ranks.bit_length() - 1, groups.bit_length() - 1
    assert ranks == 1 << steps and groups == 1 << flips and steps >= 3 and rows % (ranks * CHUNKS) == 0

    def shape(*dims, dtype=F32):
        return jax.ShapeDtypeStruct(dims, dtype)

    def swap(x, step):
        return lax.ppermute(x, "tm", [(i, i ^ (1 << order(i & 1, steps)[step])) for i in range(ranks)])

    me = lax.axis_index("tm").astype(jnp.int32).reshape(1)
    tail = lax.ppermute(loadings, "tm", [(i, i + 1) for i in range(ranks - 1)])
    flat = motifs.reshape(rows * motif_count, lags)
    depth, rest = motif_count * lags, frames - lags
    macs = rows * depth * frames * 3
    mh, ml, rh, rl, numer, head_counts, own_loads, total = call(
        body_kernel,
        [shape(rows, depth, dtype=BF16)] * 2 + [shape(rows, rest, dtype=BF16)] * 2
        + [shape(rows + ONES, depth), shape(rows, lags), shape(motif_count, frames), shape(motif_count, lags)],
        me, *(pltpu.with_memory_space_constraint(x, pltpu.HBM) for x in (counts, flat, loadings)),
        spaces=[pltpu.HBM] * 3,
        scratch=[pltpu.VMEM((rows * motif_count, lags), F32), pltpu.VMEM((rows, rest), F32)]
        + [pltpu.VMEM((depth, rest), BF16)] * 2 + [pltpu.SemaphoreType.DMA((4,))],
        limit=BODY_LIMIT, flops=4 * macs,
    )
    half = rows // CHUNKS // 2
    sizes = [half + 1] + [half] * (CHUNKS - 1)
    parts = [shape(size * motif_count, lags) for size in sizes]
    *send, fh, fl, hh, hl, denom = call(
        functools.partial(head_kernel, CHUNKS),
        parts + [shape(rows, lags, dtype=BF16)] * 2 + [shape(depth, lags, dtype=BF16)] * 2 + [shape(motif_count, lags)],
        me, tail, head_counts, own_loads, mh, ml, numer, limit=6,
    )

    def cube(x):
        return x.reshape(-1, motif_count, lags)

    got = [swap(cube(x), 0) for x in send]
    keep = call(
        functools.partial(home_kernel, CHUNKS), parts, me, fh, fl, hh, hl, denom, numer, limit=6, flops=macs // 4
    )
    keep = [cube(x) for x in keep]
    part, ahead = call(
        lagged_kernel, [shape(motif_count, frames), shape(motif_count, lags)], me, mh, ml, fh, fl, rh, rl,
        scratch=[pltpu.VMEM((rows, depth), BF16)] * 2, limit=8, flops=2 * macs,
    )

    for step in range(1, steps - 1):
        half //= 2
        for c in range(CHUNKS):
            sums = [shape(half + (c == 0), motif_count, lags)] * 2
            send[c], keep[c] = call(
                functools.partial(fold_kernel, step, steps, half), sums, me, keep[c], got[c]
            )
            got[c] = swap(send[c], step)
        if step == 1:
            got[0], part, ahead = lax.optimization_barrier((got[0], part, ahead))
        if step == 2:
            ahead = lax.ppermute(ahead, "tm", [(i, i - 1) for i in range(1, ranks)])
            (part,) = call(halo_kernel, [shape(motif_count, frames + lags)], me, part, ahead, total)
            got[0], part = lax.optimization_barrier((got[0], part))
    for c in range(CHUNKS):
        (keep[c],) = call(pair_kernel, [shape(half + (c == 0), motif_count, lags)], me, keep[c], got[c])
        got[c] = swap(keep[c], steps - 1)
    other = jnp.zeros_like(part)
    for flip in range(flips):
        if flip:
            (part,) = call(pair_kernel, [part], me, part, other)
        other = lax.ppermute(part, "neur", [(i, i ^ (1 << flip)) for i in range(groups)])
    (new_loadings,) = call(
        functools.partial(loads_kernel, ranks), [shape(motif_count, frames)], me, part, other, own_loads
    )
    got[0], new_loadings = lax.optimization_barrier((got[0], new_loadings))
    mine = [None] * CHUNKS
    for c in range(CHUNKS):
        mine[c], *more = call(
            functools.partial(update_kernel, c, steps), [shape(half, motif_count, lags)] + [shape(motif_count, lags)] * (c == 0),
            me, keep[c], got[c], denom, motifs,
        )
        if more:
            denom = more[0]
    for step in range(steps - 2, 0, -1):
        for c in range(CHUNKS):
            got[c] = swap(mine[c], step)
        half *= 2
        for c in range(CHUNKS):
            (mine[c],) = call(
                functools.partial(join_kernel, step, steps), [shape(half, motif_count, lags)], me, mine[c], got[c]
            )
    out = None
    waiting = []
    for c in range(CHUNKS):
        got[c] = swap(mine[c], 0)
        waiting.append(((c * half * 2, True), mine[c]))
        out = store(me, out, motifs, waiting)
        waiting = [((c * half * 2, False), got[c])]
    return store(me, out, motifs, waiting), new_loadings


def store(me, out, like, waiting):
    places, blocks = zip(*waiting)
    given = [] if out is None else [out]
    (out,) = call(
        functools.partial(store_kernel, places), [jax.ShapeDtypeStruct(like.shape, F32)], me, *blocks, *given,
        spaces=[pltpu.VMEM] * len(blocks) + [pltpu.HBM] * len(given), outs=[pltpu.HBM],
        scratch=[pltpu.SemaphoreType.DMA((len(blocks),))], aliases={len(blocks) + 1: 0} if given else None,
    )
    return out


def solution(mesh):
    in_specs = (P("neur", "tm"), P("neur", None, None), P(None, "tm"))
    out_specs = (P("neur", None, None), P(None, "tm"))
    return jax.shard_map(body, mesh=mesh, in_specs=in_specs, out_specs=out_specs, check_vma=False)
```

```python
import functools
import math

import jax
import jax.numpy as jnp
from jax import lax
from jax.experimental import pallas as pl
from jax.experimental.pallas import tpu as pltpu
from jax.sharding import PartitionSpec as P

F32, BF16 = jnp.float32, jnp.bfloat16
NN = (((1,), (0,)), ((), ()))
NT = (((1,), (1,)), ((), ()))
TN = (((0,), (0,)), ((), ()))
MIB = 1024 * 1024
BODY_LIMIT = 20
ONES = 16
LOADS_AFTER = 0
PARTS = (1, 1)


def split(x):
    high = x.astype(BF16)
    return high, (x - high.astype(F32)).astype(BF16)


def dot3(ah, al, bh, bl, dims):
    def dot(a, b):
        return lax.dot_general(a, b, dims, preferred_element_type=F32)

    return dot(ah, bh) + (dot(ah, bl) + dot(al, bh))


def toeplitz(row, lags):
    return pltpu.roll(jnp.broadcast_to(row, (lags, row.shape[1])), 0, 1, stride=1, stride_axis=0)


def place(me, step, steps):
    first, second = (order(core, steps)[step] for core in range(2))
    return jnp.where(me & 1 == 0, (me >> first) & 1, (me >> second) & 1)


def order(core, steps):
    return [0, 2, 1, *range(3, steps)] if core else list(range(steps))


class Chain:
    def __init__(self, me):
        self.me, self.token = me, None

    def __call__(self, kernel, out_shapes, *args, limit=4, spaces=None, outs=None, scratch=(), aliases=None, flops=0,
                 order=True):
        spaces = spaces or [pltpu.VMEM] * len(args)
        outs = outs or [pltpu.VMEM] * len(out_shapes)
        aliases, tokens = dict(aliases or {}), []
        if order and self.token is not None:
            tokens = [self.token]
            aliases[len(args) + 1] = len(out_shapes)
        given, results = 1 + len(args), len(out_shapes)

        def run(*refs):
            inputs, rest = refs[:given], refs[given + len(tokens):]
            kernel(*inputs, *rest[:results], *rest[results + len(tokens):])

        made = pl.pallas_call(
            run,
            out_shape=[*out_shapes, *(jax.ShapeDtypeStruct(t.shape, t.dtype) for t in tokens)],
            in_specs=[pl.BlockSpec(memory_space=space) for space in [pltpu.SMEM, *spaces, *[pltpu.VMEM] * len(tokens)]],
            out_specs=[pl.BlockSpec(memory_space=space) for space in [*outs, *[pltpu.VMEM] * len(tokens)]],
            scratch_shapes=list(scratch),
            input_output_aliases=aliases,
            compiler_params=pltpu.CompilerParams(vmem_limit_bytes=int(limit * MIB)),
            cost_estimate=pl.CostEstimate(flops=flops, bytes_accessed=0, transcendentals=0),
            name=getattr(kernel, "func", kernel).__name__,
        )(self.me, *args, *tokens)
        if tokens:
            self.token = made[-1]
        return made[:results]


def body_kernel(me_ref, counts_hbm, motifs_hbm, loads_hbm, mh_ref, ml_ref, rh_ref, rl_ref, numer_ref, counts_ref,
                loads_ref, total_ref, motifs_ref, rest_ref, th, tl, sems):
    rows, frames = counts_hbm.shape
    motif_count = loads_ref.shape[0]
    lags = counts_ref.shape[1]
    copies = [
        pltpu.make_async_copy(loads_hbm, loads_ref, sems.at[0]),
        pltpu.make_async_copy(motifs_hbm, motifs_ref, sems.at[1]),
        pltpu.make_async_copy(counts_hbm.at[:, pl.ds(lags, frames - lags)], rest_ref, sems.at[2]),
        pltpu.make_async_copy(counts_hbm.at[:, pl.ds(0, lags)], counts_ref, sems.at[3]),
    ]
    for copy in copies:
        copy.start()
    copies[0].wait()
    for k in range(motif_count):
        at = pl.ds(k * lags, lags)
        th[at, :], tl[at, :] = split(toeplitz(loads_ref[pl.ds(k, 1), :], lags)[:, lags:])
    copies[1].wait()
    for k in range(motif_count):
        at = pl.ds(k * lags, lags)
        mh_ref[:, at], ml_ref[:, at] = split(motifs_ref[pl.ds(k, rows, stride=motif_count), :])
    estimate = dot3(mh_ref[...], ml_ref[...], th[...], tl[...], NN)
    copies[2].wait()
    rh_ref[...], rl_ref[...] = split(rest_ref[...] / estimate)
    ones = jnp.ones((ONES, frames - lags), BF16)
    xh = jnp.concatenate([rh_ref[...], ones], axis=0)
    xl = jnp.concatenate([rl_ref[...], jnp.zeros_like(ones)], axis=0)
    for k in range(0, motif_count, 2):
        at = pl.ds(k * lags, 2 * lags)
        numer_ref[:, at] = dot3(xh, xl, th[at, :], tl[at, :], NT)
    total_ref[...] = jnp.sum(motifs_ref[...].reshape(rows, motif_count, lags), axis=0)
    copies[3].wait()


def numer_rows(numer, motif_count, out_ref, count):
    lags = out_ref.shape[-1]
    for k in range(motif_count):
        out_ref[pl.ds(k, count, stride=motif_count), :] = numer[:count, k * lags:(k + 1) * lags]


def blocks(sizes, core):
    at = [sum(sizes[:c]) for c in range(len(sizes))]
    step = math.gcd(*sizes) // 2
    return [pl.ds(pl.multiple_of(first + core * (size // 2), step), size // 2) for first, size in zip(at, sizes)]


def slabs(numer, sizes):
    return [numer[sum(sizes[:c]) // 2:sum(sizes[:c + 1]) // 2] for c in range(len(sizes))]


def head_kernel(sizes, me_ref, tail_ref, counts_ref, loads_ref, mh_ref, ml_ref, numer_ref, *refs):
    *send_refs, fh_ref, fl_ref, hh_ref, hl_ref, denom_ref = refs
    rows, lags = counts_ref.shape
    motif_count, frames = loads_ref.shape
    for k in range(motif_count):
        at = pl.ds(k * lags, lags)
        row = jnp.concatenate([tail_ref[pl.ds(k, 1), frames - lags:], loads_ref[pl.ds(k, 1), :lags]], axis=1)
        hh_ref[at, :], hl_ref[at, :] = split(toeplitz(row, lags)[:, lags:])
    estimate = dot3(mh_ref[...], ml_ref[...], hh_ref[...], hl_ref[...], NN)
    fh_ref[...], fl_ref[...] = split(counts_ref[...] / estimate)
    away = blocks(sizes, 1 - (me_ref[0] & 1))
    ones = jnp.ones((ONES, lags), BF16)
    xh = jnp.concatenate([*(fh_ref[at, :] for at in away), ones], axis=0)
    xl = jnp.concatenate([*(fl_ref[at, :] for at in away), jnp.zeros_like(ones)], axis=0)
    for k in range(0, motif_count, 2):
        at = pl.ds(k * lags, 2 * lags)
        numer = dot3(xh, xl, hh_ref[at, :], hl_ref[at, :], NT)
        for j in range(2):
            there, here = pl.ds((k + j) * lags, lags), slice(j * lags, (j + 1) * lags)
            for ref, at, slab in zip(send_refs, away, slabs(numer, sizes)):
                ref[pl.ds(k + j, at.size, stride=motif_count), :] = slab[:, here] + numer_ref[at, there]
            denom = numer[rows // 2:rows // 2 + 1, here] + numer_ref[pl.ds(rows, 1), there]
            send_refs[0][pl.ds(away[0].size * motif_count + k + j, 1), :] = denom
            denom_ref[pl.ds(k + j, 1), :] = denom


def home_kernel(sizes, me_ref, fh_ref, fl_ref, hh_ref, hl_ref, denom_ref, numer_ref, *keep_refs):
    rows, lags = fh_ref.shape
    motif_count = denom_ref.shape[0]
    home = blocks(sizes, me_ref[0] & 1)
    xh = jnp.concatenate([fh_ref[at, :] for at in home], axis=0)
    xl = jnp.concatenate([fl_ref[at, :] for at in home], axis=0)
    for k in range(0, motif_count, 2):
        at = pl.ds(k * lags, 2 * lags)
        numer = dot3(xh, xl, hh_ref[at, :], hl_ref[at, :], NT)
        for j in range(2):
            there, here = pl.ds((k + j) * lags, lags), slice(j * lags, (j + 1) * lags)
            for ref, at, slab in zip(keep_refs, home, slabs(numer, sizes)):
                ref[pl.ds(k + j, at.size, stride=motif_count), :] = slab[:, here] + numer_ref[at, there]
    keep_refs[0][pl.ds(home[0].size * motif_count, motif_count), :] = denom_ref[...]


def fold_kernel(step, steps, half, me_ref, mine_ref, got_ref, send_ref, keep_ref):
    bit = place(me_ref[0], step, steps)
    for out, part in ((send_ref, 1 - bit), (keep_ref, bit)):
        at = pl.ds(part * half, half)
        out[:half] = mine_ref[at] + got_ref[at]
        if out.shape[0] > half:
            out[half:] = mine_ref[2 * half:] + got_ref[2 * half:]


def pair_kernel(me_ref, mine_ref, got_ref, out_ref):
    out_ref[...] = mine_ref[...] + got_ref[...]


def pair_row_kernel(me_ref, mine_ref, got_ref, row_ref, out_ref):
    rows = mine_ref.shape[0]
    out_ref[:rows] = mine_ref[...] + got_ref[...]
    out_ref[rows] = row_ref[...]


def carry(me, bit, mine, got):
    return jnp.where(me & ((1 << bit) - 1) == 0, got, mine)


def carry_bit(me, step, steps):
    first, second = (order(core, steps)[step] for core in range(2))
    return jnp.where(me & 1 == 0, first, second)


def update_kernel(first, size, steps, me_ref, mine_ref, got_ref, denom_ref, motifs_ref, out_ref, *denom_out):
    rows, at, me = size >> (steps - 1), first, me_ref[0]
    for step in range(steps - 1):
        size //= 2
        at = at + place(me, step, steps) * size
    numer = mine_ref[:rows] + got_ref[:rows]
    if denom_out:
        denom = mine_ref[rows] + got_ref[rows]
        denom_out[0][...] = denom
        out_ref[rows] = carry(me, steps - 1, mine_ref[rows + 1], got_ref[rows + 1])
    else:
        denom = denom_ref[...]
    out_ref[:rows] = motifs_ref[pl.ds(at, rows)] * numer / denom[None]


def join_kernel(step, steps, half, me_ref, mine_ref, got_ref, out_ref):
    me = me_ref[0]
    bit = place(me, step, steps)
    out_ref[pl.ds(bit * half, half)] = mine_ref[:half]
    out_ref[pl.ds((1 - bit) * half, half)] = got_ref[:half]
    if mine_ref.shape[0] > half:
        out_ref[2 * half] = carry(me, carry_bit(me, step, steps), mine_ref[half], got_ref[half])


def store_kernel(parts, row_at, ranks, me_ref, *refs):
    refs, sems = refs[:-1], refs[-1]
    core = me_ref[0] & 1
    copies = []
    out_hbm = refs[-1] if row_at is None else refs[-3]
    for i, ((at, rows, own), block) in enumerate(zip(parts, refs)):
        at = at + (core if own else 1 - core) * rows
        copies.append(pltpu.make_async_copy(block.at[pl.ds(0, rows)], out_hbm.at[pl.ds(at, rows)], sems.at[i]))
    for copy in copies:
        copy.start()
    if row_at is not None:
        block, (numer_ref, scale_ref) = refs[0], refs[len(parts):len(parts) + 2]
        loads_hbm, loads_ref = refs[-2:]
        frames, lags = numer_ref.shape[1], block.shape[-1]
        rest = frames - lags
        ahead = jnp.where(me_ref[0] == ranks - 1, 0.0, block[row_at])
        loads_ref[:, :rest] = scale_ref[:, :rest] * numer_ref[:, :rest]
        loads_ref[:, rest:] = scale_ref[:, rest:] * (numer_ref[:, rest:] + ahead)
        copies.append(pltpu.make_async_copy(loads_ref, loads_hbm, sems.at[len(parts)]))
        copies[-1].start()
    for copy in copies:
        copy.wait()


def lagged_kernel(me_ref, mh_ref, ml_ref, fh_ref, fl_ref, rh_ref, rl_ref, total_ref, out_ref, ph, pw):
    motif_count, lags = total_ref.shape
    frames = out_ref.shape[1] - 2 * lags
    width = frames + lags
    down = lax.broadcasted_iota(jnp.int32, (lags, lags), 0)
    across = lax.broadcasted_iota(jnp.int32, (lags, lags), 1)
    flip = (down + across == lags - 1).astype(BF16)
    xh = jnp.concatenate([fh_ref[...], rh_ref[...]], axis=1)
    xl = jnp.concatenate([fl_ref[...], rl_ref[...]], axis=1)
    for k in range(motif_count):
        at = pl.ds(k * lags, lags)
        for ref, out in ((mh_ref, ph), (ml_ref, pw)):
            out[:, at] = lax.dot_general(ref[:, at], flip, NN, preferred_element_type=F32).astype(BF16)
    for k in range(0, motif_count, 4):
        at = pl.ds(k * lags, 4 * lags)
        lagged = dot3(ph[:, at], pw[:, at], xh, xl, TN)
        for j in range(4):
            wide = jnp.concatenate([jnp.zeros((lags, lags), F32), lagged[j * lags:(j + 1) * lags]], axis=1)
            skewed = pltpu.roll(wide, width - (lags - 1), 1, stride=1, stride_axis=0)
            numer = jnp.sum(skewed, axis=0, keepdims=True)
            out_ref[pl.ds(k + j, 1), :frames] = numer[:, lags:]
            out_ref[pl.ds(k + j, 1), frames:width] = numer[:, :lags]
    out_ref[:, width:] = total_ref[...]


def loads_kernel(ranks, me_ref, mine_ref, got_ref, loads_ref, ahead_ref, numer_ref, scale_ref):
    frames, lags = loads_ref.shape[1], ahead_ref.shape[1]
    both = mine_ref[...] + got_ref[...]
    numer_ref[...] = both[:, :frames]
    ahead_ref[...] = both[:, frames:frames + lags]
    left = (ranks - me_ref[0]) * frames
    lag = lax.broadcasted_iota(jnp.int32, (lags, frames), 0)
    frame = lax.broadcasted_iota(jnp.int32, (lags, frames), 1)
    valid = (lag + frame < left).astype(F32)
    total = both[:, frames + lags:]
    denom = lax.dot_general(total, valid, NN, precision=lax.Precision.HIGHEST, preferred_element_type=F32)
    scale_ref[...] = loads_ref[...] / denom


def body(counts, motifs, loadings):
    rows, motif_count, lags = motifs.shape
    frames = loadings.shape[1]
    ranks, groups = lax.axis_size("tm"), lax.axis_size("neur")
    steps, flips = ranks.bit_length() - 1, groups.bit_length() - 1
    assert ranks == 1 << steps and groups == 1 << flips and steps >= 3

    def shape(*dims, dtype=F32):
        return jax.ShapeDtypeStruct(dims, dtype)

    def swap(x, step):
        return lax.ppermute(x, "tm", [(i, i ^ (1 << order(i & 1, steps)[step])) for i in range(ranks)])

    call = Chain(lax.axis_index("tm").astype(jnp.int32).reshape(1))
    tail = lax.ppermute(loadings, "tm", [(i, i + 1) for i in range(ranks - 1)])
    flat = motifs.reshape(rows * motif_count, lags)
    depth, rest = motif_count * lags, frames - lags
    macs = rows * depth * frames * 3
    mh, ml, rh, rl, numer, head_counts, own_loads, total = call(
        body_kernel,
        [shape(rows, depth, dtype=BF16)] * 2 + [shape(rows, rest, dtype=BF16)] * 2
        + [shape(rows + ONES, depth), shape(rows, lags), shape(motif_count, frames), shape(motif_count, lags)],
        *(pltpu.with_memory_space_constraint(x, pltpu.HBM) for x in (counts, flat, loadings)),
        spaces=[pltpu.HBM] * 3,
        scratch=[pltpu.VMEM((rows * motif_count, lags), F32), pltpu.VMEM((rows, rest), F32)]
        + [pltpu.VMEM((depth, rest), BF16)] * 2 + [pltpu.SemaphoreType.DMA((4,))],
        limit=BODY_LIMIT, flops=4 * macs,
    )
    sizes = [rows * share // sum(PARTS) for share in PARTS]
    assert sum(sizes) == rows and all(size % (ranks // 2) == 0 for size in sizes)
    chunks = range(len(sizes))
    half = [size // 2 for size in sizes]
    extra = [int(c == 0) for c in chunks]
    parts = [shape((half[c] + extra[c]) * motif_count, lags) for c in chunks]
    *send, fh, fl, hh, hl, denom = call(
        functools.partial(head_kernel, sizes),
        parts + [shape(rows, lags, dtype=BF16)] * 2 + [shape(depth, lags, dtype=BF16)] * 2 + [shape(motif_count, lags)],
        tail, head_counts, own_loads, mh, ml, numer, limit=6,
    )

    call.token = denom

    def cube(x):
        return x.reshape(-1, motif_count, lags)

    def cubes(count):
        return shape(count, motif_count, lags)

    got = [swap(cube(x), 0) for x in send]
    keep = call(
        functools.partial(home_kernel, sizes), parts, fh, fl, hh, hl, denom, numer, limit=6, flops=macs // 4
    )
    keep = [cube(x) for x in keep]
    (part,) = call(
        lagged_kernel, [shape(motif_count, frames + 2 * lags)], mh, ml, fh, fl, rh, rl, total,
        scratch=[pltpu.VMEM((rows, depth), BF16)] * 2, limit=8, flops=2 * macs,
    )
    other = jnp.zeros_like(part)
    for flip in range(flips):
        if flip:
            (part,) = call(pair_kernel, [part], part, other, order=False)
        other = lax.ppermute(part, "neur", [(i, i ^ (1 << flip)) for i in range(groups)])
    for step in range(1, steps - 1):
        for c in chunks:
            half[c] //= 2
            send[c], keep[c] = call(
                functools.partial(fold_kernel, step, steps, half[c]), [cubes(half[c] + extra[c])] * 2, keep[c], got[c]
            )
            got[c] = swap(send[c], step)
            if step == 2 and c == LOADS_AFTER:
                ahead, numer, scale = call(
                    functools.partial(loads_kernel, ranks), [shape(motif_count, lags)] + [shape(motif_count, frames)] * 2,
                    part, other, own_loads,
                )
    for c in chunks:
        if c == 0:
            (keep[c],) = call(pair_row_kernel, [cubes(half[c] + 2)], keep[c], got[c], ahead)
        else:
            (keep[c],) = call(pair_kernel, [cubes(half[c])], keep[c], got[c])
        got[c] = swap(keep[c], steps - 1)
    mine = [None for c in chunks]
    for c in chunks:
        mine[c], *more = call(
            functools.partial(update_kernel, sum(sizes[:c]), sizes[c], steps),
            [cubes(half[c] + extra[c])] + [shape(motif_count, lags)] * extra[c], keep[c], got[c], denom, motifs,
        )
        if more:
            denom = more[0]
        got[c] = swap(mine[c], steps - 2)
    out, new_loadings, waiting = None, None, []
    for step in range(steps - 2, 0, -1):
        for c in chunks:
            (mine[c],) = call(
                functools.partial(join_kernel, step, steps, half[c]), [cubes(2 * half[c] + extra[c])], mine[c], got[c]
            )
            half[c] *= 2
            got[c] = swap(mine[c], step - 1)
            if step == 1:
                waiting.append((sum(sizes[:c]), half[c], True, mine[c]))
                out, new_loadings = store(call, out, new_loadings, rows, waiting, numer, scale, ranks)
                waiting = [(sum(sizes[:c]), half[c], False, got[c])]
    out, new_loadings = store(call, out, new_loadings, rows, waiting, numer, scale, ranks)
    return out, new_loadings


def store(call, out, new_loadings, rows, waiting, numer, scale, ranks):
    waiting = sorted(waiting, key=lambda block: block[2])
    first, half, own, block = waiting[0]
    brings = first == 0 and not own
    given = [block for *_, block in waiting] + [numer, scale] * brings
    spaces = [pltpu.VMEM] * len(given)
    results = [jax.ShapeDtypeStruct((rows, *block.shape[1:]), F32)] + [jax.ShapeDtypeStruct(numer.shape, F32)] * brings
    aliases = {}
    if out is not None:
        given.append(out)
        spaces.append(pltpu.HBM)
        aliases = {len(given): 0}
    out, *more = call(
        functools.partial(store_kernel, [place[:3] for place in waiting], half if brings else None, ranks),
        results, *given, spaces=spaces, outs=[pltpu.HBM] * len(results), aliases=aliases,
        scratch=[pltpu.VMEM(numer.shape, F32)] * brings + [pltpu.SemaphoreType.DMA((3,))],
    )
    return out, more[0] if brings else new_loadings


def solution(mesh):
    in_specs = (P("neur", "tm"), P("neur", None, None), P(None, "tm"))
    out_specs = (P("neur", None, None), P(None, "tm"))
    return jax.shard_map(body, mesh=mesh, in_specs=in_specs, out_specs=out_specs, check_vma=False)
```

```python
import functools
import math

import jax
import jax.numpy as jnp
from jax import lax
from jax.experimental import pallas as pl
from jax.experimental.pallas import tpu as pltpu
from jax.sharding import PartitionSpec as P

F32, BF16 = jnp.float32, jnp.bfloat16
NN = (((1,), (0,)), ((), ()))
NT = (((1,), (1,)), ((), ()))
TN = (((0,), (0,)), ((), ()))
MIB = 1024 * 1024
BODY_LIMIT = 20
ONES = 16
LOADS_AFTER = 0
PARTS = (1, 1)


def split(x):
    high = x.astype(BF16)
    return high, (x - high.astype(F32)).astype(BF16)


def dot3(ah, al, bh, bl, dims):
    def dot(a, b):
        return lax.dot_general(a, b, dims, preferred_element_type=F32)

    return dot(ah, bh) + (dot(ah, bl) + dot(al, bh))


def toeplitz(row, lags):
    return pltpu.roll(jnp.broadcast_to(row, (lags, row.shape[1])), 0, 1, stride=1, stride_axis=0)


def place(me, step, steps):
    first, second = (order(core, steps)[step] for core in range(2))
    return jnp.where(me & 1 == 0, (me >> first) & 1, (me >> second) & 1)


def order(core, steps):
    return [0, 2, 1, *range(3, steps)] if core else list(range(steps))


class Chain:
    def __init__(self, me):
        self.me, self.token = me, None

    def __call__(self, kernel, out_shapes, *args, limit=4, spaces=None, outs=None, scratch=(), aliases=None, flops=0,
                 order=True):
        spaces = spaces or [pltpu.VMEM] * len(args)
        outs = outs or [pltpu.VMEM] * len(out_shapes)
        aliases, tokens = dict(aliases or {}), []
        if order and self.token is not None:
            tokens = [self.token]
            aliases[len(args) + 1] = len(out_shapes)
        given, results = 1 + len(args), len(out_shapes)

        def run(*refs):
            inputs, rest = refs[:given], refs[given + len(tokens):]
            kernel(*inputs, *rest[:results], *rest[results + len(tokens):])

        made = pl.pallas_call(
            run,
            out_shape=[*out_shapes, *(jax.ShapeDtypeStruct(t.shape, t.dtype) for t in tokens)],
            in_specs=[pl.BlockSpec(memory_space=space) for space in [pltpu.SMEM, *spaces, *[pltpu.VMEM] * len(tokens)]],
            out_specs=[pl.BlockSpec(memory_space=space) for space in [*outs, *[pltpu.VMEM] * len(tokens)]],
            scratch_shapes=list(scratch),
            input_output_aliases=aliases,
            compiler_params=pltpu.CompilerParams(vmem_limit_bytes=int(limit * MIB)),
            cost_estimate=pl.CostEstimate(flops=flops, bytes_accessed=0, transcendentals=0),
            name=getattr(kernel, "func", kernel).__name__,
        )(self.me, *args, *tokens)
        if tokens:
            self.token = made[-1]
        return made[:results]


def body_kernel(me_ref, counts_hbm, motifs_hbm, loads_hbm, mh_ref, ml_ref, rh_ref, rl_ref, numer_ref, counts_ref,
                loads_ref, total_ref, motifs_ref, rest_ref, th, tl, sems):
    rows, frames = counts_hbm.shape
    motif_count = loads_ref.shape[0]
    lags = counts_ref.shape[1]
    copies = [
        pltpu.make_async_copy(loads_hbm, loads_ref, sems.at[0]),
        pltpu.make_async_copy(motifs_hbm, motifs_ref, sems.at[1]),
        pltpu.make_async_copy(counts_hbm.at[:, pl.ds(lags, frames - lags)], rest_ref, sems.at[2]),
        pltpu.make_async_copy(counts_hbm.at[:, pl.ds(0, lags)], counts_ref, sems.at[3]),
    ]
    for copy in copies:
        copy.start()
    copies[0].wait()
    for k in range(motif_count):
        at = pl.ds(k * lags, lags)
        th[at, :], tl[at, :] = split(toeplitz(loads_ref[pl.ds(k, 1), :], lags)[:, lags:])
    copies[1].wait()
    for k in range(motif_count):
        at = pl.ds(k * lags, lags)
        mh_ref[:, at], ml_ref[:, at] = split(motifs_ref[pl.ds(k, rows, stride=motif_count), :])
    estimate = dot3(mh_ref[...], ml_ref[...], th[...], tl[...], NN)
    copies[2].wait()
    rh_ref[...], rl_ref[...] = split(rest_ref[...] / estimate)
    ones = jnp.ones((ONES, frames - lags), BF16)
    xh = jnp.concatenate([rh_ref[...], ones], axis=0)
    xl = jnp.concatenate([rl_ref[...], jnp.zeros_like(ones)], axis=0)
    for k in range(0, motif_count, 2):
        at = pl.ds(k * lags, 2 * lags)
        numer_ref[:, at] = dot3(xh, xl, th[at, :], tl[at, :], NT)
    total_ref[...] = jnp.sum(motifs_ref[...].reshape(rows, motif_count, lags), axis=0)
    copies[3].wait()


def numer_rows(numer, motif_count, out_ref, count):
    lags = out_ref.shape[-1]
    for k in range(motif_count):
        out_ref[pl.ds(k, count, stride=motif_count), :] = numer[:count, k * lags:(k + 1) * lags]


def blocks(sizes, core):
    at = [sum(sizes[:c]) for c in range(len(sizes))]
    step = math.gcd(*sizes) // 2
    return [pl.ds(pl.multiple_of(first + core * (size // 2), step), size // 2) for first, size in zip(at, sizes)]


def slabs(numer, sizes):
    return [numer[sum(sizes[:c]) // 2:sum(sizes[:c + 1]) // 2] for c in range(len(sizes))]


def head_kernel(sizes, me_ref, tail_ref, counts_ref, loads_ref, mh_ref, ml_ref, numer_ref, *refs):
    *send_refs, fh_ref, fl_ref, hh_ref, hl_ref, denom_ref = refs
    rows, lags = counts_ref.shape
    motif_count, frames = loads_ref.shape
    for k in range(motif_count):
        at = pl.ds(k * lags, lags)
        tail = jnp.where(me_ref[0] == 0, 0.0, tail_ref[pl.ds(k, 1), frames - lags:])
        row = jnp.concatenate([tail, loads_ref[pl.ds(k, 1), :lags]], axis=1)
        hh_ref[at, :], hl_ref[at, :] = split(toeplitz(row, lags)[:, lags:])
    estimate = dot3(mh_ref[...], ml_ref[...], hh_ref[...], hl_ref[...], NN)
    fh_ref[...], fl_ref[...] = split(counts_ref[...] / estimate)
    away = blocks(sizes, 1 - (me_ref[0] & 1))
    ones = jnp.ones((ONES, lags), BF16)
    xh = jnp.concatenate([*(fh_ref[at, :] for at in away), ones], axis=0)
    xl = jnp.concatenate([*(fl_ref[at, :] for at in away), jnp.zeros_like(ones)], axis=0)
    for k in range(0, motif_count, 2):
        at = pl.ds(k * lags, 2 * lags)
        numer = dot3(xh, xl, hh_ref[at, :], hl_ref[at, :], NT)
        for j in range(2):
            there, here = pl.ds((k + j) * lags, lags), slice(j * lags, (j + 1) * lags)
            for ref, at, slab in zip(send_refs, away, slabs(numer, sizes)):
                ref[pl.ds(k + j, at.size, stride=motif_count), :] = slab[:, here] + numer_ref[at, there]
            denom = numer[rows // 2:rows // 2 + 1, here] + numer_ref[pl.ds(rows, 1), there]
            send_refs[0][pl.ds(away[0].size * motif_count + k + j, 1), :] = denom
            denom_ref[pl.ds(k + j, 1), :] = denom


def home_kernel(sizes, me_ref, fh_ref, fl_ref, hh_ref, hl_ref, denom_ref, numer_ref, *keep_refs):
    rows, lags = fh_ref.shape
    motif_count = denom_ref.shape[0]
    home = blocks(sizes, me_ref[0] & 1)
    xh = jnp.concatenate([fh_ref[at, :] for at in home], axis=0)
    xl = jnp.concatenate([fl_ref[at, :] for at in home], axis=0)
    for k in range(0, motif_count, 2):
        at = pl.ds(k * lags, 2 * lags)
        numer = dot3(xh, xl, hh_ref[at, :], hl_ref[at, :], NT)
        for j in range(2):
            there, here = pl.ds((k + j) * lags, lags), slice(j * lags, (j + 1) * lags)
            for ref, at, slab in zip(keep_refs, home, slabs(numer, sizes)):
                ref[pl.ds(k + j, at.size, stride=motif_count), :] = slab[:, here] + numer_ref[at, there]
    keep_refs[0][pl.ds(home[0].size * motif_count, motif_count), :] = denom_ref[...]


def fold_kernel(step, steps, half, me_ref, mine_ref, got_ref, send_ref, keep_ref):
    bit = place(me_ref[0], step, steps)
    for out, part in ((send_ref, 1 - bit), (keep_ref, bit)):
        at = pl.ds(part * half, half)
        out[:half] = mine_ref[at] + got_ref[at]
        if out.shape[0] > half:
            out[half:] = mine_ref[2 * half:] + got_ref[2 * half:]


def pair_kernel(me_ref, mine_ref, got_ref, out_ref):
    out_ref[...] = mine_ref[...] + got_ref[...]


def pair_row_kernel(me_ref, mine_ref, got_ref, row_ref, out_ref):
    rows = mine_ref.shape[0]
    out_ref[:rows] = mine_ref[...] + got_ref[...]
    out_ref[rows] = row_ref[...]


def carry(me, bit, mine, got):
    return jnp.where(me & ((1 << bit) - 1) == 0, got, mine)


def carry_bit(me, step, steps):
    first, second = (order(core, steps)[step] for core in range(2))
    return jnp.where(me & 1 == 0, first, second)


def update_kernel(first, size, steps, me_ref, mine_ref, got_ref, denom_ref, motifs_ref, out_ref, *denom_out):
    rows, at, me = size >> (steps - 1), first, me_ref[0]
    for step in range(steps - 1):
        size //= 2
        at = at + place(me, step, steps) * size
    numer = mine_ref[:rows] + got_ref[:rows]
    if denom_out:
        denom = mine_ref[rows] + got_ref[rows]
        denom_out[0][...] = denom
        out_ref[rows] = carry(me, steps - 1, mine_ref[rows + 1], got_ref[rows + 1])
    else:
        denom = denom_ref[...]
    out_ref[:rows] = motifs_ref[pl.ds(at, rows)] * numer / denom[None]


def join_kernel(step, steps, half, me_ref, mine_ref, got_ref, out_ref):
    me = me_ref[0]
    bit = place(me, step, steps)
    out_ref[pl.ds(bit * half, half)] = mine_ref[:half]
    out_ref[pl.ds((1 - bit) * half, half)] = got_ref[:half]
    if mine_ref.shape[0] > half:
        out_ref[2 * half] = carry(me, carry_bit(me, step, steps), mine_ref[half], got_ref[half])


def store_kernel(parts, row_at, ranks, me_ref, *refs):
    refs, sems = refs[:-1], refs[-1]
    core = me_ref[0] & 1
    copies = []
    out_hbm = refs[-1] if row_at is None else refs[-3]
    for i, ((at, rows, own), block) in enumerate(zip(parts, refs)):
        at = at + (core if own else 1 - core) * rows
        copies.append(pltpu.make_async_copy(block.at[pl.ds(0, rows)], out_hbm.at[pl.ds(at, rows)], sems.at[i]))
    for copy in copies:
        copy.start()
    if row_at is not None:
        block, (numer_ref, scale_ref) = refs[0], refs[len(parts):len(parts) + 2]
        loads_hbm, loads_ref = refs[-2:]
        frames, lags = numer_ref.shape[1], block.shape[-1]
        rest = frames - lags
        ahead = jnp.where(me_ref[0] == ranks - 1, 0.0, block[row_at])
        loads_ref[:, :rest] = scale_ref[:, :rest] * numer_ref[:, :rest]
        loads_ref[:, rest:] = scale_ref[:, rest:] * (numer_ref[:, rest:] + ahead)
        copies.append(pltpu.make_async_copy(loads_ref, loads_hbm, sems.at[len(parts)]))
        copies[-1].start()
    for copy in copies:
        copy.wait()


def lagged_kernel(me_ref, mh_ref, ml_ref, fh_ref, fl_ref, rh_ref, rl_ref, total_ref, out_ref, ph, pw):
    motif_count, lags = total_ref.shape
    frames = out_ref.shape[1] - 2 * lags
    width = frames + lags
    down = lax.broadcasted_iota(jnp.int32, (lags, lags), 0)
    across = lax.broadcasted_iota(jnp.int32, (lags, lags), 1)
    flip = (down + across == lags - 1).astype(BF16)
    xh = jnp.concatenate([fh_ref[...], rh_ref[...]], axis=1)
    xl = jnp.concatenate([fl_ref[...], rl_ref[...]], axis=1)
    for k in range(motif_count):
        at = pl.ds(k * lags, lags)
        for ref, out in ((mh_ref, ph), (ml_ref, pw)):
            out[:, at] = lax.dot_general(ref[:, at], flip, NN, preferred_element_type=F32).astype(BF16)
    for k in range(0, motif_count, 4):
        at = pl.ds(k * lags, 4 * lags)
        lagged = dot3(ph[:, at], pw[:, at], xh, xl, TN)
        for j in range(4):
            wide = jnp.concatenate([jnp.zeros((lags, lags), F32), lagged[j * lags:(j + 1) * lags]], axis=1)
            skewed = pltpu.roll(wide, width - (lags - 1), 1, stride=1, stride_axis=0)
            numer = jnp.sum(skewed, axis=0, keepdims=True)
            out_ref[pl.ds(k + j, 1), :frames] = numer[:, lags:]
            out_ref[pl.ds(k + j, 1), frames:width] = numer[:, :lags]
    out_ref[:, width:] = total_ref[...]


def loads_kernel(ranks, me_ref, mine_ref, got_ref, loads_ref, ahead_ref, numer_ref, scale_ref):
    frames, lags = loads_ref.shape[1], ahead_ref.shape[1]
    both = mine_ref[...] + got_ref[...]
    numer_ref[...] = both[:, :frames]
    ahead_ref[...] = both[:, frames:frames + lags]
    left = (ranks - me_ref[0]) * frames
    lag = lax.broadcasted_iota(jnp.int32, (lags, frames), 0)
    frame = lax.broadcasted_iota(jnp.int32, (lags, frames), 1)
    valid = (lag + frame < left).astype(F32)
    total = both[:, frames + lags:]
    denom = lax.dot_general(total, valid, NN, precision=lax.Precision.HIGHEST, preferred_element_type=F32)
    scale_ref[...] = loads_ref[...] / denom


def body(counts, motifs, loadings):
    rows, motif_count, lags = motifs.shape
    frames = loadings.shape[1]
    ranks, groups = lax.axis_size("tm"), lax.axis_size("neur")
    steps, flips = ranks.bit_length() - 1, groups.bit_length() - 1
    assert ranks == 1 << steps and groups == 1 << flips and steps >= 3

    def shape(*dims, dtype=F32):
        return jax.ShapeDtypeStruct(dims, dtype)

    def swap(x, step):
        return lax.ppermute(x, "tm", [(i, i ^ (1 << order(i & 1, steps)[step])) for i in range(ranks)])

    call = Chain(lax.axis_index("tm").astype(jnp.int32).reshape(1))
    tail = lax.ppermute(loadings, "tm", [(i, (i + 1) % ranks) for i in range(ranks)])
    flat = motifs.reshape(rows * motif_count, lags)
    depth, rest = motif_count * lags, frames - lags
    macs = rows * depth * frames * 3
    mh, ml, rh, rl, numer, head_counts, own_loads, total = call(
        body_kernel,
        [shape(rows, depth, dtype=BF16)] * 2 + [shape(rows, rest, dtype=BF16)] * 2
        + [shape(rows + ONES, depth), shape(rows, lags), shape(motif_count, frames), shape(motif_count, lags)],
        *(pltpu.with_memory_space_constraint(x, pltpu.HBM) for x in (counts, flat, loadings)),
        spaces=[pltpu.HBM] * 3,
        scratch=[pltpu.VMEM((rows * motif_count, lags), F32), pltpu.VMEM((rows, rest), F32)]
        + [pltpu.VMEM((depth, rest), BF16)] * 2 + [pltpu.SemaphoreType.DMA((4,))],
        limit=BODY_LIMIT, flops=4 * macs,
    )
    sizes = [rows * share // sum(PARTS) for share in PARTS]
    assert sum(sizes) == rows and all(size % (ranks // 2) == 0 for size in sizes)
    chunks = range(len(sizes))
    half = [size // 2 for size in sizes]
    extra = [int(c == 0) for c in chunks]
    parts = [shape((half[c] + extra[c]) * motif_count, lags) for c in chunks]
    *send, fh, fl, hh, hl, denom = call(
        functools.partial(head_kernel, sizes),
        parts + [shape(rows, lags, dtype=BF16)] * 2 + [shape(depth, lags, dtype=BF16)] * 2 + [shape(motif_count, lags)],
        tail, head_counts, own_loads, mh, ml, numer, limit=6,
    )

    call.token = denom

    def cube(x):
        return x.reshape(-1, motif_count, lags)

    def cubes(count):
        return shape(count, motif_count, lags)

    got = [swap(cube(x), 0) for x in send]
    keep = call(
        functools.partial(home_kernel, sizes), parts, fh, fl, hh, hl, denom, numer, limit=6, flops=macs // 4
    )
    keep = [cube(x) for x in keep]
    (part,) = call(
        lagged_kernel, [shape(motif_count, frames + 2 * lags)], mh, ml, fh, fl, rh, rl, total,
        scratch=[pltpu.VMEM((rows, depth), BF16)] * 2, limit=8, flops=2 * macs,
    )
    other = jnp.zeros_like(part)
    for flip in range(flips):
        if flip:
            (part,) = call(pair_kernel, [part], part, other, order=False)
        other = lax.ppermute(part, "neur", [(i, i ^ (1 << flip)) for i in range(groups)])
    for step in range(1, steps - 1):
        for c in chunks:
            half[c] //= 2
            send[c], keep[c] = call(
                functools.partial(fold_kernel, step, steps, half[c]), [cubes(half[c] + extra[c])] * 2, keep[c], got[c]
            )
            got[c] = swap(send[c], step)
            if step == 2 and c == LOADS_AFTER:
                ahead, numer, scale = call(
                    functools.partial(loads_kernel, ranks), [shape(motif_count, lags)] + [shape(motif_count, frames)] * 2,
                    part, other, own_loads,
                )
    for c in chunks:
        if c == 0:
            (keep[c],) = call(pair_row_kernel, [cubes(half[c] + 2)], keep[c], got[c], ahead)
        else:
            (keep[c],) = call(pair_kernel, [cubes(half[c])], keep[c], got[c])
        got[c] = swap(keep[c], steps - 1)
    mine = [None for c in chunks]
    for c in chunks:
        mine[c], *more = call(
            functools.partial(update_kernel, sum(sizes[:c]), sizes[c], steps),
            [cubes(half[c] + extra[c])] + [shape(motif_count, lags)] * extra[c], keep[c], got[c], denom, motifs,
        )
        if more:
            denom = more[0]
        got[c] = swap(mine[c], steps - 2)
    out, new_loadings, waiting = None, None, []
    for step in range(steps - 2, 0, -1):
        for c in chunks:
            (mine[c],) = call(
                functools.partial(join_kernel, step, steps, half[c]), [cubes(2 * half[c] + extra[c])], mine[c], got[c]
            )
            half[c] *= 2
            got[c] = swap(mine[c], step - 1)
            if step == 1:
                waiting.append((sum(sizes[:c]), half[c], True, mine[c]))
                out, new_loadings = store(call, out, new_loadings, rows, waiting, numer, scale, ranks)
                waiting = [(sum(sizes[:c]), half[c], False, got[c])]
    out, new_loadings = store(call, out, new_loadings, rows, waiting, numer, scale, ranks)
    return out, new_loadings


def store(call, out, new_loadings, rows, waiting, numer, scale, ranks):
    waiting = sorted(waiting, key=lambda block: block[2])
    first, half, own, block = waiting[0]
    brings = first == 0 and not own
    given = [block for *_, block in waiting] + [numer, scale] * brings
    spaces = [pltpu.VMEM] * len(given)
    results = [jax.ShapeDtypeStruct((rows, *block.shape[1:]), F32)] + [jax.ShapeDtypeStruct(numer.shape, F32)] * brings
    aliases = {}
    if out is not None:
        given.append(out)
        spaces.append(pltpu.HBM)
        aliases = {len(given): 0}
    out, *more = call(
        functools.partial(store_kernel, [place[:3] for place in waiting], half if brings else None, ranks),
        results, *given, spaces=spaces, outs=[pltpu.HBM] * len(results), aliases=aliases,
        scratch=[pltpu.VMEM(numer.shape, F32)] * brings + [pltpu.SemaphoreType.DMA((3,))],
    )
    return out, more[0] if brings else new_loadings


def solution(mesh):
    in_specs = (P("neur", "tm"), P("neur", None, None), P(None, "tm"))
    out_specs = (P("neur", None, None), P(None, "tm"))
    return jax.shard_map(body, mesh=mesh, in_specs=in_specs, out_specs=out_specs, check_vma=False)
```

```python
import functools
import math

import jax
import jax.numpy as jnp
from jax import lax
from jax.experimental import pallas as pl
from jax.experimental.pallas import tpu as pltpu
from jax.sharding import PartitionSpec as P

F32, BF16 = jnp.float32, jnp.bfloat16
NN = (((1,), (0,)), ((), ()))
NT = (((1,), (1,)), ((), ()))
TN = (((0,), (0,)), ((), ()))
MIB = 1024 * 1024
BODY_LIMIT = 20
ONES = 16
PARTS = (1, 1)


def split(x):
    high = x.astype(BF16)
    return high, (x - high.astype(F32)).astype(BF16)


def dot3(ah, al, bh, bl, dims):
    def dot(a, b):
        return lax.dot_general(a, b, dims, preferred_element_type=F32)

    return dot(ah, bh) + (dot(ah, bl) + dot(al, bh))


def toeplitz(row, lags):
    return pltpu.roll(jnp.broadcast_to(row, (lags, row.shape[1])), 0, 1, stride=1, stride_axis=0)


def place(me, step, steps):
    first, second = (order(core, steps)[step] for core in range(2))
    return jnp.where(me & 1 == 0, (me >> first) & 1, (me >> second) & 1)


def order(core, steps):
    return [0, 2, 1, *range(3, steps)] if core else list(range(steps))


class Chain:
    def __init__(self, me):
        self.me, self.token = me, None

    def __call__(self, kernel, out_shapes, *args, limit=4, spaces=None, outs=None, scratch=(), aliases=None, flops=0,
                 order=True):
        spaces = spaces or [pltpu.VMEM] * len(args)
        outs = outs or [pltpu.VMEM] * len(out_shapes)
        aliases, tokens = dict(aliases or {}), []
        if order and self.token is not None:
            tokens = [self.token]
            aliases[len(args) + 1] = len(out_shapes)
        given, results = 1 + len(args), len(out_shapes)

        def run(*refs):
            inputs, rest = refs[:given], refs[given + len(tokens):]
            kernel(*inputs, *rest[:results], *rest[results + len(tokens):])

        made = pl.pallas_call(
            run,
            out_shape=[*out_shapes, *(jax.ShapeDtypeStruct(t.shape, t.dtype) for t in tokens)],
            in_specs=[pl.BlockSpec(memory_space=space) for space in [pltpu.SMEM, *spaces, *[pltpu.VMEM] * len(tokens)]],
            out_specs=[pl.BlockSpec(memory_space=space) for space in [*outs, *[pltpu.VMEM] * len(tokens)]],
            scratch_shapes=list(scratch),
            input_output_aliases=aliases,
            compiler_params=pltpu.CompilerParams(vmem_limit_bytes=int(limit * MIB)),
            cost_estimate=pl.CostEstimate(flops=flops, bytes_accessed=0, transcendentals=0),
            name=getattr(kernel, "func", kernel).__name__,
        )(self.me, *args, *tokens)
        if tokens:
            self.token = made[-1]
        return made[:results]


def open_kernel(me_ref, out_ref):
    out_ref[...] = jnp.zeros_like(out_ref)


def body_kernel(me_ref, counts_ref, motifs_ref, loads_ref, mh_ref, ml_ref, rh_ref, rl_ref, numer_ref, total_ref, th, tl):
    rows, frames = counts_ref.shape
    motif_count, lags = total_ref.shape
    for k in range(motif_count):
        at = pl.ds(k * lags, lags)
        th[at, :], tl[at, :] = split(toeplitz(loads_ref[pl.ds(k, 1), :], lags)[:, lags:])
        mh_ref[:, at], ml_ref[:, at] = split(motifs_ref[pl.ds(k, rows, stride=motif_count), :])
    estimate = dot3(mh_ref[...], ml_ref[...], th[...], tl[...], NN)
    rh_ref[...], rl_ref[...] = split(counts_ref[:, lags:] / estimate)
    ones = jnp.ones((ONES, frames - lags), BF16)
    xh = jnp.concatenate([rh_ref[...], ones], axis=0)
    xl = jnp.concatenate([rl_ref[...], jnp.zeros_like(ones)], axis=0)
    for k in range(0, motif_count, 2):
        at = pl.ds(k * lags, 2 * lags)
        numer_ref[:, at] = dot3(xh, xl, th[at, :], tl[at, :], NT)
    total_ref[...] = jnp.sum(motifs_ref[...].reshape(rows, motif_count, lags), axis=0)


def blocks(sizes, core):
    at = [sum(sizes[:c]) for c in range(len(sizes))]
    step = math.gcd(*sizes) // 2
    return [pl.ds(pl.multiple_of(first + core * (size // 2), step), size // 2) for first, size in zip(at, sizes)]


def slabs(numer, sizes):
    return [numer[sum(sizes[:c]) // 2:sum(sizes[:c + 1]) // 2] for c in range(len(sizes))]


def head_kernel(sizes, me_ref, tail_ref, counts_ref, loads_ref, mh_ref, ml_ref, numer_ref, *refs):
    *send_refs, fh_ref, fl_ref, hh_ref, hl_ref, denom_ref = refs
    rows, frames = counts_ref.shape
    motif_count, lags = denom_ref.shape
    for k in range(motif_count):
        at = pl.ds(k * lags, lags)
        tail = jnp.where(me_ref[0] == 0, 0.0, tail_ref[pl.ds(k, 1), frames - lags:])
        row = jnp.concatenate([tail, loads_ref[pl.ds(k, 1), :lags]], axis=1)
        hh_ref[at, :], hl_ref[at, :] = split(toeplitz(row, lags)[:, lags:])
    estimate = dot3(mh_ref[...], ml_ref[...], hh_ref[...], hl_ref[...], NN)
    fh_ref[...], fl_ref[...] = split(counts_ref[:, :lags] / estimate)
    away = blocks(sizes, 1 - (me_ref[0] & 1))
    ones = jnp.ones((ONES, lags), BF16)
    xh = jnp.concatenate([*(fh_ref[at, :] for at in away), ones], axis=0)
    xl = jnp.concatenate([*(fl_ref[at, :] for at in away), jnp.zeros_like(ones)], axis=0)
    for k in range(0, motif_count, 2):
        at = pl.ds(k * lags, 2 * lags)
        numer = dot3(xh, xl, hh_ref[at, :], hl_ref[at, :], NT)
        for j in range(2):
            there, here = pl.ds((k + j) * lags, lags), slice(j * lags, (j + 1) * lags)
            for ref, at, slab in zip(send_refs, away, slabs(numer, sizes)):
                ref[pl.ds(k + j, at.size, stride=motif_count), :] = slab[:, here] + numer_ref[at, there]
            denom = numer[rows // 2:rows // 2 + 1, here] + numer_ref[pl.ds(rows, 1), there]
            send_refs[0][pl.ds(away[0].size * motif_count + k + j, 1), :] = denom
            denom_ref[pl.ds(k + j, 1), :] = denom


def home_kernel(sizes, me_ref, fh_ref, fl_ref, hh_ref, hl_ref, denom_ref, numer_ref, *keep_refs):
    rows, lags = fh_ref.shape
    motif_count = denom_ref.shape[0]
    home = blocks(sizes, me_ref[0] & 1)
    xh = jnp.concatenate([fh_ref[at, :] for at in home], axis=0)
    xl = jnp.concatenate([fl_ref[at, :] for at in home], axis=0)
    for k in range(0, motif_count, 2):
        at = pl.ds(k * lags, 2 * lags)
        numer = dot3(xh, xl, hh_ref[at, :], hl_ref[at, :], NT)
        for j in range(2):
            there, here = pl.ds((k + j) * lags, lags), slice(j * lags, (j + 1) * lags)
            for ref, at, slab in zip(keep_refs, home, slabs(numer, sizes)):
                ref[pl.ds(k + j, at.size, stride=motif_count), :] = slab[:, here] + numer_ref[at, there]
    keep_refs[0][pl.ds(home[0].size * motif_count, motif_count), :] = denom_ref[...]


def fold_kernel(step, steps, half, me_ref, mine_ref, got_ref, send_ref, keep_ref):
    bit = place(me_ref[0], step, steps)
    for out, part in ((send_ref, 1 - bit), (keep_ref, bit)):
        at = pl.ds(part * half, half)
        out[:half] = mine_ref[at] + got_ref[at]
        if out.shape[0] > half:
            out[half:] = mine_ref[2 * half:] + got_ref[2 * half:]


def pair_kernel(me_ref, mine_ref, got_ref, out_ref):
    out_ref[...] = mine_ref[...] + got_ref[...]


def pair_row_kernel(me_ref, mine_ref, got_ref, row_ref, out_ref):
    rows = mine_ref.shape[0]
    out_ref[:rows] = mine_ref[...] + got_ref[...]
    out_ref[rows] = row_ref[...]


def carry(me, bit, mine, got):
    return jnp.where(me & ((1 << bit) - 1) == 0, got, mine)


def carry_bit(me, step, steps):
    first, second = (order(core, steps)[step] for core in range(2))
    return jnp.where(me & 1 == 0, first, second)


def update_kernel(first, size, steps, me_ref, mine_ref, got_ref, denom_ref, motifs_ref, out_ref, *denom_out):
    rows, at, me = size >> (steps - 1), first, me_ref[0]
    for step in range(steps - 1):
        size //= 2
        at = at + place(me, step, steps) * size
    numer = mine_ref[:rows] + got_ref[:rows]
    if denom_out:
        denom = mine_ref[rows] + got_ref[rows]
        denom_out[0][...] = denom
    else:
        denom = denom_ref[...]
    at_row = mine_ref.shape[0] - 1
    row = carry(me, steps - 1, mine_ref[at_row], got_ref[at_row])
    for i in range(rows, out_ref.shape[0]):
        out_ref[i] = row
    out_ref[:rows] = motifs_ref[pl.ds(at, rows)] * numer / denom[None]


def join_kernel(step, steps, half, me_ref, mine_ref, got_ref, out_ref):
    me = me_ref[0]
    bit = place(me, step, steps)
    out_ref[pl.ds(bit * half, half)] = mine_ref[:half]
    out_ref[pl.ds((1 - bit) * half, half)] = got_ref[:half]
    row = carry(me, carry_bit(me, step, steps), mine_ref[half], got_ref[half])
    for i in range(2 * half, out_ref.shape[0]):
        out_ref[i] = row


def store_kernel(parts, row_at, ranks, me_ref, *refs):
    refs, sems = refs[:-1], refs[-1]
    core = me_ref[0] & 1
    copies = []
    out_hbm = refs[-1] if row_at is None else refs[-3]
    for i, ((at, rows, own), block) in enumerate(zip(parts, refs)):
        at = at + (core if own else 1 - core) * rows
        copies.append(pltpu.make_async_copy(block.at[pl.ds(0, rows)], out_hbm.at[pl.ds(at, rows)], sems.at[i]))
    for copy in copies:
        copy.start()
    if row_at is not None:
        block, (numer_ref, scale_ref) = refs[0], refs[len(parts):len(parts) + 2]
        loads_hbm, loads_ref = refs[-2:]
        frames, lags = numer_ref.shape[1], block.shape[-1]
        rest = frames - lags
        ahead = jnp.where(me_ref[0] == ranks - 1, 0.0, block[row_at])
        loads_ref[:, :rest] = scale_ref[:, :rest] * numer_ref[:, :rest]
        loads_ref[:, rest:] = scale_ref[:, rest:] * (numer_ref[:, rest:] + ahead)
        copies.append(pltpu.make_async_copy(loads_ref, loads_hbm, sems.at[len(parts)]))
        copies[-1].start()
    for copy in copies:
        copy.wait()


def lagged_kernel(me_ref, mh_ref, ml_ref, fh_ref, fl_ref, rh_ref, rl_ref, total_ref, out_ref, ph, pw):
    motif_count, lags = total_ref.shape
    frames = out_ref.shape[1] - 2 * lags
    width = frames + lags
    down = lax.broadcasted_iota(jnp.int32, (lags, lags), 0)
    across = lax.broadcasted_iota(jnp.int32, (lags, lags), 1)
    flip = (down + across == lags - 1).astype(BF16)
    xh = jnp.concatenate([fh_ref[...], rh_ref[...]], axis=1)
    xl = jnp.concatenate([fl_ref[...], rl_ref[...]], axis=1)
    for k in range(motif_count):
        at = pl.ds(k * lags, lags)
        for ref, out in ((mh_ref, ph), (ml_ref, pw)):
            out[:, at] = lax.dot_general(ref[:, at], flip, NN, preferred_element_type=F32).astype(BF16)
    for k in range(0, motif_count, 4):
        at = pl.ds(k * lags, 4 * lags)
        lagged = dot3(ph[:, at], pw[:, at], xh, xl, TN)
        for j in range(4):
            wide = jnp.concatenate([jnp.zeros((lags, lags), F32), lagged[j * lags:(j + 1) * lags]], axis=1)
            skewed = pltpu.roll(wide, width - (lags - 1), 1, stride=1, stride_axis=0)
            numer = jnp.sum(skewed, axis=0, keepdims=True)
            out_ref[pl.ds(k + j, 1), :frames] = numer[:, lags:]
            out_ref[pl.ds(k + j, 1), frames:width] = numer[:, :lags]
    out_ref[:, width:] = total_ref[...]


def loads_kernel(ranks, me_ref, mine_ref, got_ref, loads_ref, ahead_ref, numer_ref, scale_ref):
    frames, lags = loads_ref.shape[1], ahead_ref.shape[1]
    both = mine_ref[...] + got_ref[...]
    numer_ref[...] = both[:, :frames]
    ahead_ref[...] = both[:, frames:frames + lags]
    left = (ranks - me_ref[0]) * frames
    lag = lax.broadcasted_iota(jnp.int32, (lags, frames), 0)
    frame = lax.broadcasted_iota(jnp.int32, (lags, frames), 1)
    valid = (lag + frame < left).astype(F32)
    total = both[:, frames + lags:]
    denom = lax.dot_general(total, valid, NN, precision=lax.Precision.HIGHEST, preferred_element_type=F32)
    scale_ref[...] = loads_ref[...] / denom


def body(counts, motifs, loadings):
    rows, motif_count, lags = motifs.shape
    frames = loadings.shape[1]
    ranks, groups = lax.axis_size("tm"), lax.axis_size("neur")
    steps, flips = ranks.bit_length() - 1, groups.bit_length() - 1
    assert ranks == 1 << steps and groups == 1 << flips and steps >= 3

    def shape(*dims, dtype=F32):
        return jax.ShapeDtypeStruct(dims, dtype)

    def swap(x, step):
        return lax.ppermute(x, "tm", [(i, i ^ (1 << order(i & 1, steps)[step])) for i in range(ranks)])

    call = Chain(lax.axis_index("tm").astype(jnp.int32).reshape(1))
    flat = motifs.reshape(rows * motif_count, lags)
    depth, rest = motif_count * lags, frames - lags
    macs = rows * depth * frames * 3
    (call.token,) = call(open_kernel, [shape(motif_count, lags)], flops=10 ** 10)
    call.token, sent = lax.optimization_barrier((call.token, loadings))
    tail = lax.ppermute(sent, "tm", [(i, (i + 1) % ranks) for i in range(ranks)])
    mh, ml, rh, rl, numer, total = call(
        body_kernel,
        [shape(rows, depth, dtype=BF16)] * 2 + [shape(rows, rest, dtype=BF16)] * 2
        + [shape(rows + ONES, depth), shape(motif_count, lags)],
        counts, flat, loadings, scratch=[pltpu.VMEM((depth, rest), BF16)] * 2, limit=BODY_LIMIT, flops=4 * macs,
    )
    head_counts, own_loads = counts, loadings
    sizes = [rows * share // sum(PARTS) for share in PARTS]
    assert sum(sizes) == rows and all(size % (ranks // 2) == 0 for size in sizes)
    chunks = range(len(sizes))
    half = [size // 2 for size in sizes]
    extra = [int(c == 0) for c in chunks]
    parts = [shape((half[c] + extra[c]) * motif_count, lags) for c in chunks]
    *send, fh, fl, hh, hl, denom = call(
        functools.partial(head_kernel, sizes),
        parts + [shape(rows, lags, dtype=BF16)] * 2 + [shape(depth, lags, dtype=BF16)] * 2 + [shape(motif_count, lags)],
        tail, head_counts, own_loads, mh, ml, numer, limit=6,
    )


    def cube(x):
        return x.reshape(-1, motif_count, lags)

    def cubes(count):
        return shape(count, motif_count, lags)

    got = [swap(cube(x), 0) for x in send]
    keep = call(
        functools.partial(home_kernel, sizes), parts, fh, fl, hh, hl, denom, numer, limit=6, flops=macs // 4
    )
    keep = [cube(x) for x in keep]
    for step in range(1, steps - 1):
        for c in chunks:
            half[c] //= 2
            send[c], keep[c] = call(
                functools.partial(fold_kernel, step, steps, half[c]), [cubes(half[c] + extra[c])] * 2, keep[c], got[c]
            )
            got[c] = swap(send[c], step)
        if step == 1:
            (part,) = call(
                lagged_kernel, [shape(motif_count, frames + 2 * lags)], mh, ml, fh, fl, rh, rl, total,
                scratch=[pltpu.VMEM((rows, depth), BF16)] * 2, limit=8, flops=2 * macs,
            )
            other = jnp.zeros_like(part)
            for flip in range(flips):
                if flip:
                    (part,) = call(pair_kernel, [part], part, other, order=False)
                other = lax.ppermute(part, "neur", [(i, i ^ (1 << flip)) for i in range(groups)])
    last = chunks[-1]
    for c in chunks:
        if c == last:
            ahead, numer, scale = call(
                functools.partial(loads_kernel, ranks), [shape(motif_count, lags)] + [shape(motif_count, frames)] * 2,
                part, other, own_loads,
            )
            (keep[c],) = call(pair_row_kernel, [cubes(half[c] + extra[c] + 1)], keep[c], got[c], ahead)
        else:
            (keep[c],) = call(pair_row_kernel, [cubes(half[c] + extra[c] + 1)], keep[c], got[c], denom)
        got[c] = swap(keep[c], steps - 1)
    carried = [1 + (c != last) for c in chunks]
    mine = [None for c in chunks]
    for c in chunks:
        mine[c], *more = call(
            functools.partial(update_kernel, sum(sizes[:c]), sizes[c], steps),
            [cubes(half[c] + carried[c])] + [shape(motif_count, lags)] * extra[c], keep[c], got[c], denom, motifs,
        )
        if more:
            denom = more[0]
        got[c] = swap(mine[c], steps - 2)
    out, new_loadings, waiting = None, None, []
    for step in range(steps - 2, 0, -1):
        for c in chunks:
            (mine[c],) = call(
                functools.partial(join_kernel, step, steps, half[c]), [cubes(2 * half[c] + carried[c])], mine[c], got[c]
            )
            half[c] *= 2
            got[c] = swap(mine[c], step - 1)
            if step == 1:
                waiting.append((sum(sizes[:c]), half[c], True, mine[c]))
                out, new_loadings = store(call, out, new_loadings, rows, waiting, numer, scale, ranks)
                waiting = [(sum(sizes[:c]), half[c], False, got[c])]
    out, new_loadings = store(call, out, new_loadings, rows, waiting, numer, scale, ranks)
    return out, new_loadings


def store(call, out, new_loadings, rows, waiting, numer, scale, ranks):
    waiting = sorted(waiting, key=lambda block: block[2])
    first, half, own, block = waiting[0]
    brings = len(waiting) == 1 and not own
    given = [block for *_, block in waiting] + [numer, scale] * brings
    spaces = [pltpu.VMEM] * len(given)
    results = [jax.ShapeDtypeStruct((rows, *block.shape[1:]), F32)] + [jax.ShapeDtypeStruct(numer.shape, F32)] * brings
    aliases = {}
    if out is not None:
        given.append(out)
        spaces.append(pltpu.HBM)
        aliases = {len(given): 0}
    out, *more = call(
        functools.partial(store_kernel, [place[:3] for place in waiting], half if brings else None, ranks),
        results, *given, spaces=spaces, outs=[pltpu.HBM] * len(results), aliases=aliases,
        scratch=[pltpu.VMEM(numer.shape, F32)] * brings + [pltpu.SemaphoreType.DMA((3,))],
    )
    return out, more[0] if brings else new_loadings


def solution(mesh):
    in_specs = (P("neur", "tm"), P("neur", None, None), P(None, "tm"))
    out_specs = (P("neur", None, None), P(None, "tm"))
    return jax.shard_map(body, mesh=mesh, in_specs=in_specs, out_specs=out_specs, check_vma=False)
```

```python
import functools
import math

import jax
import jax.numpy as jnp
from jax import lax
from jax.experimental import pallas as pl
from jax.experimental.pallas import tpu as pltpu
from jax.sharding import PartitionSpec as P

F32, BF16 = jnp.float32, jnp.bfloat16
NN = (((1,), (0,)), ((), ()))
NT = (((1,), (1,)), ((), ()))
TN = (((0,), (0,)), ((), ()))
MIB = 1024 * 1024
BODY_LIMIT = 20
ONES = 16
PARTS = (1, 1)


def split(x):
    high = x.astype(BF16)
    return high, (x - high.astype(F32)).astype(BF16)


def dot3(ah, al, bh, bl, dims):
    def dot(a, b):
        return lax.dot_general(a, b, dims, preferred_element_type=F32)

    return dot(ah, bh) + (dot(ah, bl) + dot(al, bh))


def toeplitz(row, lags):
    return pltpu.roll(jnp.broadcast_to(row, (lags, row.shape[1])), 0, 1, stride=1, stride_axis=0)


def place(me, step, steps):
    first, second = (order(core, steps)[step] for core in range(2))
    return jnp.where(me & 1 == 0, (me >> first) & 1, (me >> second) & 1)


def order(core, steps):
    return [0, *range(3, steps), 1, 2] if core else list(range(steps))


class Chain:
    def __init__(self, me):
        self.me, self.token = me, None

    def __call__(self, kernel, out_shapes, *args, limit=4, spaces=None, outs=None, scratch=(), aliases=None, flops=0,
                 order=True):
        spaces = spaces or [pltpu.VMEM] * len(args)
        outs = outs or [pltpu.VMEM] * len(out_shapes)
        aliases, tokens = dict(aliases or {}), []
        if order and self.token is not None:
            tokens = [self.token]
            aliases[len(args) + 1] = len(out_shapes)
        given, results = 1 + len(args), len(out_shapes)

        def run(*refs):
            inputs, rest = refs[:given], refs[given + len(tokens):]
            kernel(*inputs, *rest[:results], *rest[results + len(tokens):])

        made = pl.pallas_call(
            run,
            out_shape=[*out_shapes, *(jax.ShapeDtypeStruct(t.shape, t.dtype) for t in tokens)],
            in_specs=[pl.BlockSpec(memory_space=space) for space in [pltpu.SMEM, *spaces, *[pltpu.VMEM] * len(tokens)]],
            out_specs=[pl.BlockSpec(memory_space=space) for space in [*outs, *[pltpu.VMEM] * len(tokens)]],
            scratch_shapes=list(scratch),
            input_output_aliases=aliases,
            compiler_params=pltpu.CompilerParams(vmem_limit_bytes=int(limit * MIB)),
            cost_estimate=pl.CostEstimate(flops=flops, bytes_accessed=0, transcendentals=0),
            name=getattr(kernel, "func", kernel).__name__,
        )(self.me, *args, *tokens)
        if tokens:
            self.token = made[-1]
        return made[:results]


def open_kernel(me_ref, out_ref):
    out_ref[...] = jnp.zeros_like(out_ref)


def body_kernel(me_ref, counts_ref, motifs_ref, loads_ref, mh_ref, ml_ref, rh_ref, rl_ref, numer_ref, total_ref, th, tl):
    rows, frames = counts_ref.shape
    motif_count, lags = total_ref.shape
    for k in range(motif_count):
        at = pl.ds(k * lags, lags)
        th[at, :], tl[at, :] = split(toeplitz(loads_ref[pl.ds(k, 1), :], lags)[:, lags:])
        mh_ref[:, at], ml_ref[:, at] = split(motifs_ref[pl.ds(k, rows, stride=motif_count), :])
    estimate = dot3(mh_ref[...], ml_ref[...], th[...], tl[...], NN)
    rh_ref[...], rl_ref[...] = split(counts_ref[:, lags:] / estimate)
    ones = jnp.ones((ONES, frames - lags), BF16)
    xh = jnp.concatenate([rh_ref[...], ones], axis=0)
    xl = jnp.concatenate([rl_ref[...], jnp.zeros_like(ones)], axis=0)
    for k in range(0, motif_count, 2):
        at = pl.ds(k * lags, 2 * lags)
        numer_ref[:, at] = dot3(xh, xl, th[at, :], tl[at, :], NT)
    total_ref[...] = jnp.sum(motifs_ref[...].reshape(rows, motif_count, lags), axis=0)


def blocks(sizes, core):
    at = [sum(sizes[:c]) for c in range(len(sizes))]
    step = math.gcd(*sizes) // 2
    return [pl.ds(pl.multiple_of(first + core * (size // 2), step), size // 2) for first, size in zip(at, sizes)]


def slabs(numer, sizes):
    return [numer[sum(sizes[:c]) // 2:sum(sizes[:c + 1]) // 2] for c in range(len(sizes))]


def head_kernel(sizes, me_ref, tail_ref, counts_ref, loads_ref, mh_ref, ml_ref, numer_ref, *refs):
    *send_refs, fh_ref, fl_ref, hh_ref, hl_ref, denom_ref = refs
    rows, frames = counts_ref.shape
    motif_count, lags = denom_ref.shape
    for k in range(motif_count):
        at = pl.ds(k * lags, lags)
        tail = jnp.where(me_ref[0] == 0, 0.0, tail_ref[pl.ds(k, 1), frames - lags:])
        row = jnp.concatenate([tail, loads_ref[pl.ds(k, 1), :lags]], axis=1)
        hh_ref[at, :], hl_ref[at, :] = split(toeplitz(row, lags)[:, lags:])
    estimate = dot3(mh_ref[...], ml_ref[...], hh_ref[...], hl_ref[...], NN)
    fh_ref[...], fl_ref[...] = split(counts_ref[:, :lags] / estimate)
    away = blocks(sizes, 1 - (me_ref[0] & 1))
    ones = jnp.ones((ONES, lags), BF16)
    xh = jnp.concatenate([*(fh_ref[at, :] for at in away), ones], axis=0)
    xl = jnp.concatenate([*(fl_ref[at, :] for at in away), jnp.zeros_like(ones)], axis=0)
    for k in range(0, motif_count, 2):
        at = pl.ds(k * lags, 2 * lags)
        numer = dot3(xh, xl, hh_ref[at, :], hl_ref[at, :], NT)
        for j in range(2):
            there, here = pl.ds((k + j) * lags, lags), slice(j * lags, (j + 1) * lags)
            for ref, at, slab in zip(send_refs, away, slabs(numer, sizes)):
                ref[pl.ds(k + j, at.size, stride=motif_count), :] = slab[:, here] + numer_ref[at, there]
            denom = numer[rows // 2:rows // 2 + 1, here] + numer_ref[pl.ds(rows, 1), there]
            send_refs[0][pl.ds(away[0].size * motif_count + k + j, 1), :] = denom
            denom_ref[pl.ds(k + j, 1), :] = denom


def home_kernel(sizes, me_ref, fh_ref, fl_ref, hh_ref, hl_ref, denom_ref, numer_ref, *keep_refs):
    rows, lags = fh_ref.shape
    motif_count = denom_ref.shape[0]
    home = blocks(sizes, me_ref[0] & 1)
    xh = jnp.concatenate([fh_ref[at, :] for at in home], axis=0)
    xl = jnp.concatenate([fl_ref[at, :] for at in home], axis=0)
    for k in range(0, motif_count, 2):
        at = pl.ds(k * lags, 2 * lags)
        numer = dot3(xh, xl, hh_ref[at, :], hl_ref[at, :], NT)
        for j in range(2):
            there, here = pl.ds((k + j) * lags, lags), slice(j * lags, (j + 1) * lags)
            for ref, at, slab in zip(keep_refs, home, slabs(numer, sizes)):
                ref[pl.ds(k + j, at.size, stride=motif_count), :] = slab[:, here] + numer_ref[at, there]
    keep_refs[0][pl.ds(home[0].size * motif_count, motif_count), :] = denom_ref[...]


def fold_kernel(step, steps, half, me_ref, mine_ref, got_ref, send_ref, keep_ref):
    bit = place(me_ref[0], step, steps)
    for out, part in ((send_ref, 1 - bit), (keep_ref, bit)):
        at = pl.ds(part * half, half)
        out[:half] = mine_ref[at] + got_ref[at]
        if out.shape[0] > half:
            out[half:] = mine_ref[2 * half:] + got_ref[2 * half:]


def pair_kernel(me_ref, mine_ref, got_ref, out_ref):
    out_ref[...] = mine_ref[...] + got_ref[...]


def pair_row_kernel(me_ref, mine_ref, got_ref, row_ref, out_ref):
    rows = mine_ref.shape[0]
    out_ref[:rows] = mine_ref[...] + got_ref[...]
    out_ref[rows] = row_ref[...]


def carry(me, bit, mine, got):
    return jnp.where(me & ((1 << bit) - 1) == 0, got, mine)


def carry_bit(me, step, steps):
    first, second = (order(core, steps)[step] for core in range(2))
    return jnp.where(me & 1 == 0, first, second)


def update_kernel(first, size, steps, me_ref, mine_ref, got_ref, denom_ref, motifs_ref, out_ref, *denom_out):
    rows, at, me = size >> (steps - 1), first, me_ref[0]
    for step in range(steps - 1):
        size //= 2
        at = at + place(me, step, steps) * size
    numer = mine_ref[:rows] + got_ref[:rows]
    if denom_out:
        denom = mine_ref[rows] + got_ref[rows]
        denom_out[0][...] = denom
    else:
        denom = denom_ref[...]
    at_row = mine_ref.shape[0] - 1
    row = carry(me, steps - 1, mine_ref[at_row], got_ref[at_row])
    for i in range(rows, out_ref.shape[0]):
        out_ref[i] = row
    out_ref[:rows] = motifs_ref[pl.ds(at, rows)] * numer / denom[None]


def join_kernel(step, steps, half, me_ref, mine_ref, got_ref, out_ref):
    me = me_ref[0]
    bit = place(me, step, steps)
    out_ref[pl.ds(bit * half, half)] = mine_ref[:half]
    out_ref[pl.ds((1 - bit) * half, half)] = got_ref[:half]
    row = carry(me, carry_bit(me, step, steps), mine_ref[half], got_ref[half])
    for i in range(2 * half, out_ref.shape[0]):
        out_ref[i] = row


def store_kernel(parts, row_at, ranks, me_ref, *refs):
    refs, sems = refs[:-1], refs[-1]
    core = me_ref[0] & 1
    copies = []
    out_hbm = refs[-1] if row_at is None else refs[-3]
    for i, ((at, rows, own), block) in enumerate(zip(parts, refs)):
        at = at + (core if own else 1 - core) * rows
        copies.append(pltpu.make_async_copy(block.at[pl.ds(0, rows)], out_hbm.at[pl.ds(at, rows)], sems.at[i]))
    for copy in copies:
        copy.start()
    if row_at is not None:
        block, (numer_ref, scale_ref) = refs[0], refs[len(parts):len(parts) + 2]
        loads_hbm, loads_ref = refs[-2:]
        frames, lags = numer_ref.shape[1], block.shape[-1]
        rest = frames - lags
        ahead = jnp.where(me_ref[0] == ranks - 1, 0.0, block[row_at])
        loads_ref[:, :rest] = scale_ref[:, :rest] * numer_ref[:, :rest]
        loads_ref[:, rest:] = scale_ref[:, rest:] * (numer_ref[:, rest:] + ahead)
        copies.append(pltpu.make_async_copy(loads_ref, loads_hbm, sems.at[len(parts)]))
        copies[-1].start()
    for copy in copies:
        copy.wait()


def lagged_kernel(me_ref, mh_ref, ml_ref, fh_ref, fl_ref, rh_ref, rl_ref, total_ref, out_ref, ph, pw):
    motif_count, lags = total_ref.shape
    frames = out_ref.shape[1] - 2 * lags
    width = frames + lags
    down = lax.broadcasted_iota(jnp.int32, (lags, lags), 0)
    across = lax.broadcasted_iota(jnp.int32, (lags, lags), 1)
    flip = (down + across == lags - 1).astype(BF16)
    xh = jnp.concatenate([fh_ref[...], rh_ref[...]], axis=1)
    xl = jnp.concatenate([fl_ref[...], rl_ref[...]], axis=1)
    for k in range(motif_count):
        at = pl.ds(k * lags, lags)
        for ref, out in ((mh_ref, ph), (ml_ref, pw)):
            out[:, at] = lax.dot_general(ref[:, at], flip, NN, preferred_element_type=F32).astype(BF16)
    for k in range(0, motif_count, 4):
        at = pl.ds(k * lags, 4 * lags)
        lagged = dot3(ph[:, at], pw[:, at], xh, xl, TN)
        for j in range(4):
            wide = jnp.concatenate([jnp.zeros((lags, lags), F32), lagged[j * lags:(j + 1) * lags]], axis=1)
            skewed = pltpu.roll(wide, width - (lags - 1), 1, stride=1, stride_axis=0)
            numer = jnp.sum(skewed, axis=0, keepdims=True)
            out_ref[pl.ds(k + j, 1), :frames] = numer[:, lags:]
            out_ref[pl.ds(k + j, 1), frames:width] = numer[:, :lags]
    out_ref[:, width:] = total_ref[...]


def loads_kernel(ranks, me_ref, mine_ref, got_ref, loads_ref, ahead_ref, numer_ref, scale_ref):
    frames, lags = loads_ref.shape[1], ahead_ref.shape[1]
    both = mine_ref[...] + got_ref[...]
    numer_ref[...] = both[:, :frames]
    ahead_ref[...] = both[:, frames:frames + lags]
    left = (ranks - me_ref[0]) * frames
    lag = lax.broadcasted_iota(jnp.int32, (lags, frames), 0)
    frame = lax.broadcasted_iota(jnp.int32, (lags, frames), 1)
    valid = (lag + frame < left).astype(F32)
    total = both[:, frames + lags:]
    denom = lax.dot_general(total, valid, NN, precision=lax.Precision.HIGHEST, preferred_element_type=F32)
    scale_ref[...] = loads_ref[...] / denom


def body(counts, motifs, loadings):
    rows, motif_count, lags = motifs.shape
    frames = loadings.shape[1]
    ranks, groups = lax.axis_size("tm"), lax.axis_size("neur")
    steps, flips = ranks.bit_length() - 1, groups.bit_length() - 1
    assert ranks == 1 << steps and groups == 1 << flips and steps >= 3

    def shape(*dims, dtype=F32):
        return jax.ShapeDtypeStruct(dims, dtype)

    def swap(x, step):
        return lax.ppermute(x, "tm", [(i, i ^ (1 << order(i & 1, steps)[step])) for i in range(ranks)])

    call = Chain(lax.axis_index("tm").astype(jnp.int32).reshape(1))
    flat = motifs.reshape(rows * motif_count, lags)
    depth, rest = motif_count * lags, frames - lags
    macs = rows * depth * frames * 3
    (call.token,) = call(open_kernel, [shape(motif_count, lags)], flops=10 ** 10)
    call.token, sent = lax.optimization_barrier((call.token, loadings))
    tail = lax.ppermute(sent, "tm", [(i, (i + 1) % ranks) for i in range(ranks)])
    mh, ml, rh, rl, numer, total = call(
        body_kernel,
        [shape(rows, depth, dtype=BF16)] * 2 + [shape(rows, rest, dtype=BF16)] * 2
        + [shape(rows + ONES, depth), shape(motif_count, lags)],
        counts, flat, loadings, scratch=[pltpu.VMEM((depth, rest), BF16)] * 2, limit=BODY_LIMIT, flops=4 * macs,
    )
    head_counts, own_loads = counts, loadings
    sizes = [rows * share // sum(PARTS) for share in PARTS]
    assert sum(sizes) == rows and all(size % (ranks // 2) == 0 for size in sizes)
    chunks = range(len(sizes))
    half = [size // 2 for size in sizes]
    extra = [int(c == 0) for c in chunks]
    parts = [shape((half[c] + extra[c]) * motif_count, lags) for c in chunks]
    *send, fh, fl, hh, hl, denom = call(
        functools.partial(head_kernel, sizes),
        parts + [shape(rows, lags, dtype=BF16)] * 2 + [shape(depth, lags, dtype=BF16)] * 2 + [shape(motif_count, lags)],
        tail, head_counts, own_loads, mh, ml, numer, limit=6,
    )


    def cube(x):
        return x.reshape(-1, motif_count, lags)

    def cubes(count):
        return shape(count, motif_count, lags)

    got = [swap(cube(x), 0) for x in send]
    keep = call(
        functools.partial(home_kernel, sizes), parts, fh, fl, hh, hl, denom, numer, limit=6, flops=macs // 4
    )
    keep = [cube(x) for x in keep]
    for step in range(1, steps - 1):
        for c in chunks:
            half[c] //= 2
            send[c], keep[c] = call(
                functools.partial(fold_kernel, step, steps, half[c]), [cubes(half[c] + extra[c])] * 2, keep[c], got[c]
            )
            got[c] = swap(send[c], step)
        if step == 1:
            (part,) = call(
                lagged_kernel, [shape(motif_count, frames + 2 * lags)], mh, ml, fh, fl, rh, rl, total,
                scratch=[pltpu.VMEM((rows, depth), BF16)] * 2, limit=8, flops=2 * macs,
            )
            other = jnp.zeros_like(part)
            for flip in range(flips):
                if flip:
                    (part,) = call(pair_kernel, [part], part, other, order=False)
                other = lax.ppermute(part, "neur", [(i, i ^ (1 << flip)) for i in range(groups)])
    last = chunks[-1]
    for c in chunks:
        if c == last:
            ahead, numer, scale = call(
                functools.partial(loads_kernel, ranks), [shape(motif_count, lags)] + [shape(motif_count, frames)] * 2,
                part, other, own_loads,
            )
            (keep[c],) = call(pair_row_kernel, [cubes(half[c] + extra[c] + 1)], keep[c], got[c], ahead)
        else:
            (keep[c],) = call(pair_row_kernel, [cubes(half[c] + extra[c] + 1)], keep[c], got[c], denom)
        got[c] = swap(keep[c], steps - 1)
    carried = [1 + (c != last) for c in chunks]
    mine = [None for c in chunks]
    for c in chunks:
        mine[c], *more = call(
            functools.partial(update_kernel, sum(sizes[:c]), sizes[c], steps),
            [cubes(half[c] + carried[c])] + [shape(motif_count, lags)] * extra[c], keep[c], got[c], denom, motifs,
        )
        if more:
            denom = more[0]
        got[c] = swap(mine[c], steps - 2)
    out, new_loadings, waiting = None, None, []
    for step in range(steps - 2, 0, -1):
        for c in chunks:
            (mine[c],) = call(
                functools.partial(join_kernel, step, steps, half[c]), [cubes(2 * half[c] + carried[c])], mine[c], got[c]
            )
            half[c] *= 2
            got[c] = swap(mine[c], step - 1)
            if step == 1:
                waiting.append((sum(sizes[:c]), half[c], True, mine[c]))
                out, new_loadings = store(call, out, new_loadings, rows, waiting, numer, scale, ranks)
                waiting = [(sum(sizes[:c]), half[c], False, got[c])]
    out, new_loadings = store(call, out, new_loadings, rows, waiting, numer, scale, ranks)
    return out, new_loadings


def store(call, out, new_loadings, rows, waiting, numer, scale, ranks):
    waiting = sorted(waiting, key=lambda block: block[2])
    first, half, own, block = waiting[0]
    brings = len(waiting) == 1 and not own
    given = [block for *_, block in waiting] + [numer, scale] * brings
    spaces = [pltpu.VMEM] * len(given)
    results = [jax.ShapeDtypeStruct((rows, *block.shape[1:]), F32)] + [jax.ShapeDtypeStruct(numer.shape, F32)] * brings
    aliases = {}
    if out is not None:
        given.append(out)
        spaces.append(pltpu.HBM)
        aliases = {len(given): 0}
    out, *more = call(
        functools.partial(store_kernel, [place[:3] for place in waiting], half if brings else None, ranks),
        results, *given, spaces=spaces, outs=[pltpu.HBM] * len(results), aliases=aliases,
        scratch=[pltpu.VMEM(numer.shape, F32)] * brings + [pltpu.SemaphoreType.DMA((3,))],
    )
    return out, more[0] if brings else new_loadings


def solution(mesh):
    in_specs = (P("neur", "tm"), P("neur", None, None), P(None, "tm"))
    out_specs = (P("neur", None, None), P(None, "tm"))
    return jax.shard_map(body, mesh=mesh, in_specs=in_specs, out_specs=out_specs, check_vma=False)
```

```python
import functools
import math

import jax
import jax.numpy as jnp
from jax import lax
from jax.experimental import pallas as pl
from jax.experimental.pallas import tpu as pltpu
from jax.sharding import PartitionSpec as P

F32, BF16 = jnp.float32, jnp.bfloat16
NN = (((1,), (0,)), ((), ()))
NT = (((1,), (1,)), ((), ()))
TN = (((0,), (0,)), ((), ()))
MIB = 1024 * 1024
BODY_LIMIT = 20
ONES = 16
PARTS = (1, 1)


def split(x):
    high = x.astype(BF16)
    return high, (x - high.astype(F32)).astype(BF16)


def dot3(ah, al, bh, bl, dims):
    def dot(a, b):
        return lax.dot_general(a, b, dims, preferred_element_type=F32)

    return dot(ah, bh) + (dot(ah, bl) + dot(al, bh))


def toeplitz(row, lags):
    return pltpu.roll(jnp.broadcast_to(row, (lags, row.shape[1])), 0, 1, stride=1, stride_axis=0)


def place(me, step, steps):
    first, second = (order(core, steps)[step] for core in range(2))
    return jnp.where(me & 1 == 0, (me >> first) & 1, (me >> second) & 1)


def order(core, steps):
    return [0, *range(3, steps), 1, 2] if core else list(range(steps))


class Chain:
    def __init__(self, me):
        self.me, self.token = me, None

    def __call__(self, kernel, out_shapes, *args, limit=4, spaces=None, outs=None, scratch=(), aliases=None, flops=0,
                 order=True):
        spaces = spaces or [pltpu.VMEM] * len(args)
        outs = outs or [pltpu.VMEM] * len(out_shapes)
        aliases, tokens = dict(aliases or {}), []
        if order and self.token is not None:
            tokens = [self.token]
            aliases[len(args) + 1] = len(out_shapes)
        given, results = 1 + len(args), len(out_shapes)

        def run(*refs):
            inputs, rest = refs[:given], refs[given + len(tokens):]
            kernel(*inputs, *rest[:results], *rest[results + len(tokens):])

        made = pl.pallas_call(
            run,
            out_shape=[*out_shapes, *(jax.ShapeDtypeStruct(t.shape, t.dtype) for t in tokens)],
            in_specs=[pl.BlockSpec(memory_space=space) for space in [pltpu.SMEM, *spaces, *[pltpu.VMEM] * len(tokens)]],
            out_specs=[pl.BlockSpec(memory_space=space) for space in [*outs, *[pltpu.VMEM] * len(tokens)]],
            scratch_shapes=list(scratch),
            input_output_aliases=aliases,
            compiler_params=pltpu.CompilerParams(vmem_limit_bytes=int(limit * MIB)),
            cost_estimate=pl.CostEstimate(flops=flops, bytes_accessed=0, transcendentals=0),
            name=getattr(kernel, "func", kernel).__name__,
        )(self.me, *args, *tokens)
        if tokens:
            self.token = made[-1]
        return made[:results]


def open_kernel(me_ref, out_ref):
    out_ref[...] = jnp.zeros_like(out_ref)


def body_kernel(me_ref, counts_ref, motifs_ref, loads_ref, mh_ref, ml_ref, rh_ref, rl_ref, numer_ref, total_ref, th, tl):
    rows, frames = counts_ref.shape
    motif_count, lags = total_ref.shape
    for k in range(motif_count):
        at = pl.ds(k * lags, lags)
        th[at, :], tl[at, :] = split(toeplitz(loads_ref[pl.ds(k, 1), :], lags)[:, lags:])
        mh_ref[:, at], ml_ref[:, at] = split(motifs_ref[pl.ds(k, rows, stride=motif_count), :])
    estimate = dot3(mh_ref[...], ml_ref[...], th[...], tl[...], NN)
    rh_ref[...], rl_ref[...] = split(counts_ref[:, lags:] / estimate)
    ones = jnp.ones((ONES, frames - lags), BF16)
    xh = jnp.concatenate([rh_ref[...], ones], axis=0)
    xl = jnp.concatenate([rl_ref[...], jnp.zeros_like(ones)], axis=0)
    for k in range(0, motif_count, 2):
        at = pl.ds(k * lags, 2 * lags)
        numer_ref[:, at] = dot3(xh, xl, th[at, :], tl[at, :], NT)
    total_ref[...] = jnp.sum(motifs_ref[...].reshape(rows, motif_count, lags), axis=0)


def blocks(sizes, core):
    at = [sum(sizes[:c]) for c in range(len(sizes))]
    step = math.gcd(*sizes) // 2
    return [pl.ds(pl.multiple_of(first + core * (size // 2), step), size // 2) for first, size in zip(at, sizes)]


def slabs(numer, sizes):
    return [numer[sum(sizes[:c]) // 2:sum(sizes[:c + 1]) // 2] for c in range(len(sizes))]


def head_kernel(sizes, me_ref, tail_ref, counts_ref, loads_ref, mh_ref, ml_ref, numer_ref, *refs):
    *send_refs, fh_ref, fl_ref, hh_ref, hl_ref, denom_ref = refs
    rows, frames = counts_ref.shape
    motif_count, lags = denom_ref.shape
    for k in range(motif_count):
        at = pl.ds(k * lags, lags)
        tail = jnp.where(me_ref[0] == 0, 0.0, tail_ref[pl.ds(k, 1), frames - lags:])
        row = jnp.concatenate([tail, loads_ref[pl.ds(k, 1), :lags]], axis=1)
        hh_ref[at, :], hl_ref[at, :] = split(toeplitz(row, lags)[:, lags:])
    estimate = dot3(mh_ref[...], ml_ref[...], hh_ref[...], hl_ref[...], NN)
    fh_ref[...], fl_ref[...] = split(counts_ref[:, :lags] / estimate)
    away = blocks(sizes, 1 - (me_ref[0] & 1))
    ones = jnp.ones((ONES, lags), BF16)
    xh = jnp.concatenate([*(fh_ref[at, :] for at in away), ones], axis=0)
    xl = jnp.concatenate([*(fl_ref[at, :] for at in away), jnp.zeros_like(ones)], axis=0)
    for k in range(0, motif_count, 2):
        at = pl.ds(k * lags, 2 * lags)
        numer = dot3(xh, xl, hh_ref[at, :], hl_ref[at, :], NT)
        for j in range(2):
            there, here = pl.ds((k + j) * lags, lags), slice(j * lags, (j + 1) * lags)
            for ref, at, slab in zip(send_refs, away, slabs(numer, sizes)):
                ref[pl.ds(k + j, at.size, stride=motif_count), :] = slab[:, here] + numer_ref[at, there]
            denom = numer[rows // 2:rows // 2 + 1, here] + numer_ref[pl.ds(rows, 1), there]
            send_refs[0][pl.ds(away[0].size * motif_count + k + j, 1), :] = denom
            denom_ref[pl.ds(k + j, 1), :] = denom


def home_kernel(sizes, me_ref, fh_ref, fl_ref, hh_ref, hl_ref, denom_ref, numer_ref, *keep_refs):
    rows, lags = fh_ref.shape
    motif_count = denom_ref.shape[0]
    home = blocks(sizes, me_ref[0] & 1)
    xh = jnp.concatenate([fh_ref[at, :] for at in home], axis=0)
    xl = jnp.concatenate([fl_ref[at, :] for at in home], axis=0)
    for k in range(0, motif_count, 2):
        at = pl.ds(k * lags, 2 * lags)
        numer = dot3(xh, xl, hh_ref[at, :], hl_ref[at, :], NT)
        for j in range(2):
            there, here = pl.ds((k + j) * lags, lags), slice(j * lags, (j + 1) * lags)
            for ref, at, slab in zip(keep_refs, home, slabs(numer, sizes)):
                ref[pl.ds(k + j, at.size, stride=motif_count), :] = slab[:, here] + numer_ref[at, there]
    keep_refs[0][pl.ds(home[0].size * motif_count, motif_count), :] = denom_ref[...]


def fold_kernel(step, steps, half, me_ref, mine_ref, got_ref, send_ref, keep_ref):
    bit = place(me_ref[0], step, steps)
    for out, part in ((send_ref, 1 - bit), (keep_ref, bit)):
        at = pl.ds(part * half, half)
        out[:half] = mine_ref[at] + got_ref[at]
        if out.shape[0] > half:
            out[half:] = mine_ref[2 * half:] + got_ref[2 * half:]


def pair_kernel(me_ref, mine_ref, got_ref, out_ref):
    out_ref[...] = mine_ref[...] + got_ref[...]


def pair_row_kernel(me_ref, mine_ref, got_ref, row_ref, out_ref):
    rows = mine_ref.shape[0]
    out_ref[:rows] = mine_ref[...] + got_ref[...]
    out_ref[rows] = row_ref[...]


def carry(me, bit, mine, got):
    return jnp.where(me & ((1 << bit) - 1) == 0, got, mine)


def carry_bit(me, step, steps):
    first, second = (order(core, steps)[step] for core in range(2))
    return jnp.where(me & 1 == 0, first, second)


def update_kernel(first, size, steps, me_ref, mine_ref, got_ref, denom_ref, motifs_ref, out_ref, *denom_out):
    rows, at, me = size >> (steps - 1), first, me_ref[0]
    for step in range(steps - 1):
        size //= 2
        at = at + place(me, step, steps) * size
    numer = mine_ref[:rows] + got_ref[:rows]
    if denom_out:
        denom = mine_ref[rows] + got_ref[rows]
        denom_out[0][...] = denom
    else:
        denom = denom_ref[...]
    at_row = mine_ref.shape[0] - 1
    row = carry(me, steps - 1, mine_ref[at_row], got_ref[at_row])
    for i in range(rows, out_ref.shape[0]):
        out_ref[i] = row
    out_ref[:rows] = motifs_ref[pl.ds(at, rows)] * numer / denom[None]


def join_kernel(step, steps, size, half, me_ref, mine_ref, got_ref, out_ref):
    me = me_ref[0]
    bit = place(me, step, steps)
    for i in range(half // size):
        here = pl.ds(i * size, size)
        out_ref[pl.ds(2 * i * size + bit * size, size)] = mine_ref[here]
        out_ref[pl.ds(2 * i * size + (1 - bit) * size, size)] = got_ref[here]
    span = 1 << carry_bit(me, step, steps)
    row = jnp.where((me & (span - 1)) == span - 2, got_ref[half], mine_ref[half])
    for i in range(2 * half, out_ref.shape[0]):
        out_ref[i] = row


def store_kernel(parts, row_at, ranks, me_ref, *refs):
    refs, sems = refs[:-1], refs[-1]
    core = me_ref[0] & 1
    copies = []
    out_hbm = refs[-1] if row_at is None else refs[-3]
    for i, ((at, rows, own), block) in enumerate(zip(parts, refs)):
        at = at + (core if own else 1 - core) * rows
        copies.append(pltpu.make_async_copy(block.at[pl.ds(0, rows)], out_hbm.at[pl.ds(at, rows)], sems.at[i]))
    for copy in copies:
        copy.start()
    if row_at is not None:
        block, (numer_ref, scale_ref) = refs[0], refs[len(parts):len(parts) + 2]
        loads_hbm, loads_ref = refs[-2:]
        frames, lags = numer_ref.shape[1], block.shape[-1]
        rest = frames - lags
        ahead = jnp.where(me_ref[0] == ranks - 1, 0.0, block[row_at])
        loads_ref[:, :rest] = scale_ref[:, :rest] * numer_ref[:, :rest]
        loads_ref[:, rest:] = scale_ref[:, rest:] * (numer_ref[:, rest:] + ahead)
        copies.append(pltpu.make_async_copy(loads_ref, loads_hbm, sems.at[len(parts)]))
        copies[-1].start()
    for copy in copies:
        copy.wait()


def lagged_kernel(me_ref, mh_ref, ml_ref, fh_ref, fl_ref, rh_ref, rl_ref, total_ref, out_ref, ph, pw):
    motif_count, lags = total_ref.shape
    frames = out_ref.shape[1] - 2 * lags
    width = frames + lags
    down = lax.broadcasted_iota(jnp.int32, (lags, lags), 0)
    across = lax.broadcasted_iota(jnp.int32, (lags, lags), 1)
    flip = (down + across == lags - 1).astype(BF16)
    xh = jnp.concatenate([fh_ref[...], rh_ref[...]], axis=1)
    xl = jnp.concatenate([fl_ref[...], rl_ref[...]], axis=1)
    for k in range(motif_count):
        at = pl.ds(k * lags, lags)
        for ref, out in ((mh_ref, ph), (ml_ref, pw)):
            out[:, at] = lax.dot_general(ref[:, at], flip, NN, preferred_element_type=F32).astype(BF16)
    for k in range(0, motif_count, 4):
        at = pl.ds(k * lags, 4 * lags)
        lagged = dot3(ph[:, at], pw[:, at], xh, xl, TN)
        for j in range(4):
            wide = jnp.concatenate([jnp.zeros((lags, lags), F32), lagged[j * lags:(j + 1) * lags]], axis=1)
            skewed = pltpu.roll(wide, width - (lags - 1), 1, stride=1, stride_axis=0)
            numer = jnp.sum(skewed, axis=0, keepdims=True)
            out_ref[pl.ds(k + j, 1), :frames] = numer[:, lags:]
            out_ref[pl.ds(k + j, 1), frames:width] = numer[:, :lags]
    out_ref[:, width:] = total_ref[...]


def loads_kernel(ranks, me_ref, mine_ref, got_ref, loads_ref, ahead_ref, numer_ref, scale_ref):
    frames, lags = loads_ref.shape[1], ahead_ref.shape[1]
    both = mine_ref[...] + got_ref[...]
    numer_ref[...] = both[:, :frames]
    ahead_ref[...] = both[:, frames:frames + lags]
    left = (ranks - me_ref[0]) * frames
    lag = lax.broadcasted_iota(jnp.int32, (lags, frames), 0)
    frame = lax.broadcasted_iota(jnp.int32, (lags, frames), 1)
    valid = (lag + frame < left).astype(F32)
    total = both[:, frames + lags:]
    denom = lax.dot_general(total, valid, NN, precision=lax.Precision.HIGHEST, preferred_element_type=F32)
    scale_ref[...] = loads_ref[...] / denom


def body(counts, motifs, loadings):
    rows, motif_count, lags = motifs.shape
    frames = loadings.shape[1]
    ranks, groups = lax.axis_size("tm"), lax.axis_size("neur")
    steps, flips = ranks.bit_length() - 1, groups.bit_length() - 1
    assert ranks == 1 << steps and groups == 1 << flips and steps >= 3

    def shape(*dims, dtype=F32):
        return jax.ShapeDtypeStruct(dims, dtype)

    def swap(x, step):
        return lax.ppermute(x, "tm", [(i, i ^ (1 << order(i & 1, steps)[step])) for i in range(ranks)])

    call = Chain(lax.axis_index("tm").astype(jnp.int32).reshape(1))
    flat = motifs.reshape(rows * motif_count, lags)
    depth, rest = motif_count * lags, frames - lags
    macs = rows * depth * frames * 3
    (call.token,) = call(open_kernel, [shape(motif_count, lags)], flops=10 ** 10)
    call.token, sent = lax.optimization_barrier((call.token, loadings))
    tail = lax.ppermute(sent, "tm", [(i, (i + 1) % ranks) for i in range(ranks)])
    mh, ml, rh, rl, numer, total = call(
        body_kernel,
        [shape(rows, depth, dtype=BF16)] * 2 + [shape(rows, rest, dtype=BF16)] * 2
        + [shape(rows + ONES, depth), shape(motif_count, lags)],
        counts, flat, loadings, scratch=[pltpu.VMEM((depth, rest), BF16)] * 2, limit=BODY_LIMIT, flops=4 * macs,
    )
    head_counts, own_loads = counts, loadings
    sizes = [rows * share // sum(PARTS) for share in PARTS]
    assert sum(sizes) == rows and all(size % (ranks // 2) == 0 for size in sizes)
    chunks = range(len(sizes))
    half = [size // 2 for size in sizes]
    extra = [int(c == 0) for c in chunks]
    parts = [shape((half[c] + extra[c]) * motif_count, lags) for c in chunks]
    *send, fh, fl, hh, hl, denom = call(
        functools.partial(head_kernel, sizes),
        parts + [shape(rows, lags, dtype=BF16)] * 2 + [shape(depth, lags, dtype=BF16)] * 2 + [shape(motif_count, lags)],
        tail, head_counts, own_loads, mh, ml, numer, limit=6,
    )


    def cube(x):
        return x.reshape(-1, motif_count, lags)

    def cubes(count):
        return shape(count, motif_count, lags)

    got = [swap(cube(x), 0) for x in send]
    keep = call(
        functools.partial(home_kernel, sizes), parts, fh, fl, hh, hl, denom, numer, limit=6, flops=macs // 4
    )
    keep = [cube(x) for x in keep]
    for step in range(1, steps - 1):
        for c in chunks:
            half[c] //= 2
            send[c], keep[c] = call(
                functools.partial(fold_kernel, step, steps, half[c]), [cubes(half[c] + extra[c])] * 2, keep[c], got[c]
            )
            got[c] = swap(send[c], step)
        if step == 1:
            (part,) = call(
                lagged_kernel, [shape(motif_count, frames + 2 * lags)], mh, ml, fh, fl, rh, rl, total,
                scratch=[pltpu.VMEM((rows, depth), BF16)] * 2, limit=8, flops=2 * macs,
            )
            other = jnp.zeros_like(part)
            for flip in range(flips):
                if flip:
                    (part,) = call(pair_kernel, [part], part, other, order=False)
                other = lax.ppermute(part, "neur", [(i, i ^ (1 << flip)) for i in range(groups)])
    last = chunks[-1]
    for c in chunks:
        if c == last:
            ahead, numer, scale = call(
                functools.partial(loads_kernel, ranks), [shape(motif_count, lags)] + [shape(motif_count, frames)] * 2,
                part, other, own_loads,
            )
            (keep[c],) = call(pair_row_kernel, [cubes(half[c] + extra[c] + 1)], keep[c], got[c], ahead)
        else:
            (keep[c],) = call(pair_row_kernel, [cubes(half[c] + extra[c] + 1)], keep[c], got[c], denom)
        got[c] = swap(keep[c], steps - 1)
    carried = [1 + (c != last) for c in chunks]
    mine = [None for c in chunks]
    for c in chunks:
        mine[c], *more = call(
            functools.partial(update_kernel, sum(sizes[:c]), sizes[c], steps),
            [cubes(half[c] + carried[c])] + [shape(motif_count, lags)] * extra[c], keep[c], got[c], denom, motifs,
        )
        if more:
            denom = more[0]
        got[c] = swap(mine[c], 1)
    out, new_loadings, waiting = None, None, []
    size = list(half)
    for step in range(1, steps - 1):
        for c in chunks:
            (mine[c],) = call(
                functools.partial(join_kernel, step, steps, size[c], half[c]), [cubes(2 * half[c] + carried[c])], mine[c], got[c]
            )
            half[c] *= 2
            got[c] = swap(mine[c], (step + 1) % (steps - 1))
            if step == steps - 2:
                waiting.append((sum(sizes[:c]), half[c], True, mine[c]))
                out, new_loadings = store(call, out, new_loadings, rows, waiting, numer, scale, ranks)
                waiting = [(sum(sizes[:c]), half[c], False, got[c])]
    out, new_loadings = store(call, out, new_loadings, rows, waiting, numer, scale, ranks)
    return out, new_loadings


def store(call, out, new_loadings, rows, waiting, numer, scale, ranks):
    waiting = sorted(waiting, key=lambda block: block[2])
    first, half, own, block = waiting[0]
    brings = len(waiting) == 1 and not own
    given = [block for *_, block in waiting] + [numer, scale] * brings
    spaces = [pltpu.VMEM] * len(given)
    results = [jax.ShapeDtypeStruct((rows, *block.shape[1:]), F32)] + [jax.ShapeDtypeStruct(numer.shape, F32)] * brings
    aliases = {}
    if out is not None:
        given.append(out)
        spaces.append(pltpu.HBM)
        aliases = {len(given): 0}
    out, *more = call(
        functools.partial(store_kernel, [place[:3] for place in waiting], half if brings else None, ranks),
        results, *given, spaces=spaces, outs=[pltpu.HBM] * len(results), aliases=aliases,
        scratch=[pltpu.VMEM(numer.shape, F32)] * brings + [pltpu.SemaphoreType.DMA((3,))],
    )
    return out, more[0] if brings else new_loadings


def solution(mesh):
    in_specs = (P("neur", "tm"), P("neur", None, None), P(None, "tm"))
    out_specs = (P("neur", None, None), P(None, "tm"))
    return jax.shard_map(body, mesh=mesh, in_specs=in_specs, out_specs=out_specs, check_vma=False)
```

```python
import functools
import math

import jax
import jax.numpy as jnp
from jax import lax
from jax.experimental import pallas as pl
from jax.experimental.pallas import tpu as pltpu
from jax.sharding import PartitionSpec as P

F32, BF16 = jnp.float32, jnp.bfloat16
NN = (((1,), (0,)), ((), ()))
NT = (((1,), (1,)), ((), ()))
TN = (((0,), (0,)), ((), ()))
MIB = 1024 * 1024
BODY_LIMIT = 20
ONES = 16
PARTS = (1, 1)


def split(x):
    high = x.astype(BF16)
    return high, (x - high.astype(F32)).astype(BF16)


def dot3(ah, al, bh, bl, dims):
    def dot(a, b):
        return lax.dot_general(a, b, dims, preferred_element_type=F32)

    return dot(ah, bh) + (dot(ah, bl) + dot(al, bh))


def toeplitz(row, lags):
    return pltpu.roll(jnp.broadcast_to(row, (lags, row.shape[1])), 0, 1, stride=1, stride_axis=0)


def place(me, step, steps):
    first, second = (order(core, steps)[step] for core in range(2))
    return jnp.where(me & 1 == 0, (me >> first) & 1, (me >> second) & 1)


def order(core, steps):
    return [0, *range(3, steps), 1, 2] if core else list(range(steps))


class Chain:
    def __init__(self, me):
        self.me, self.token = me, None

    def __call__(self, kernel, out_shapes, *args, limit=4, spaces=None, outs=None, scratch=(), aliases=None, flops=0,
                 order=True):
        spaces = spaces or [pltpu.VMEM] * len(args)
        outs = outs or [pltpu.VMEM] * len(out_shapes)
        aliases, tokens = dict(aliases or {}), []
        if order and self.token is not None:
            tokens = [self.token]
            aliases[len(args) + 1] = len(out_shapes)
        given, results = 1 + len(args), len(out_shapes)

        def run(*refs):
            inputs, rest = refs[:given], refs[given + len(tokens):]
            kernel(*inputs, *rest[:results], *rest[results + len(tokens):])

        made = pl.pallas_call(
            run,
            out_shape=[*out_shapes, *(jax.ShapeDtypeStruct(t.shape, t.dtype) for t in tokens)],
            in_specs=[pl.BlockSpec(memory_space=space) for space in [pltpu.SMEM, *spaces, *[pltpu.VMEM] * len(tokens)]],
            out_specs=[pl.BlockSpec(memory_space=space) for space in [*outs, *[pltpu.VMEM] * len(tokens)]],
            scratch_shapes=list(scratch),
            input_output_aliases=aliases,
            compiler_params=pltpu.CompilerParams(vmem_limit_bytes=int(limit * MIB)),
            cost_estimate=pl.CostEstimate(flops=flops, bytes_accessed=0, transcendentals=0),
            name=getattr(kernel, "func", kernel).__name__,
        )(self.me, *args, *tokens)
        if tokens:
            self.token = made[-1]
        return made[:results]


def open_kernel(me_ref, out_ref):
    out_ref[...] = jnp.zeros_like(out_ref)


def body_kernel(me_ref, counts_ref, motifs_ref, loads_ref, mh_ref, ml_ref, rh_ref, rl_ref, numer_ref, total_ref, th, tl):
    rows, frames = counts_ref.shape
    motif_count, lags = total_ref.shape
    for k in range(motif_count):
        at = pl.ds(k * lags, lags)
        th[at, :], tl[at, :] = split(toeplitz(loads_ref[pl.ds(k, 1), :], lags)[:, lags:])
        mh_ref[:, at], ml_ref[:, at] = split(motifs_ref[pl.ds(k, rows, stride=motif_count), :])
    estimate = dot3(mh_ref[...], ml_ref[...], th[...], tl[...], NN)
    rh_ref[...], rl_ref[...] = split(counts_ref[:, lags:] / estimate)
    ones = jnp.ones((ONES, frames - lags), BF16)
    xh = jnp.concatenate([rh_ref[...], ones], axis=0)
    xl = jnp.concatenate([rl_ref[...], jnp.zeros_like(ones)], axis=0)
    for k in range(0, motif_count, 2):
        at = pl.ds(k * lags, 2 * lags)
        numer_ref[:, at] = dot3(xh, xl, th[at, :], tl[at, :], NT)
    total_ref[...] = jnp.sum(motifs_ref[...].reshape(rows, motif_count, lags), axis=0)


def blocks(sizes, core):
    at = [sum(sizes[:c]) for c in range(len(sizes))]
    step = math.gcd(*sizes) // 2
    return [pl.ds(pl.multiple_of(first + core * (size // 2), step), size // 2) for first, size in zip(at, sizes)]


def slabs(numer, sizes):
    return [numer[sum(sizes[:c]) // 2:sum(sizes[:c + 1]) // 2] for c in range(len(sizes))]


def head_kernel(sizes, me_ref, tail_ref, counts_ref, loads_ref, mh_ref, ml_ref, numer_ref, *refs):
    send_ref, fh_ref, fl_ref, hh_ref, hl_ref, denom_ref = refs
    rows, frames = counts_ref.shape
    motif_count, lags = denom_ref.shape
    for k in range(motif_count):
        at = pl.ds(k * lags, lags)
        tail = jnp.where(me_ref[0] == 0, 0.0, tail_ref[pl.ds(k, 1), frames - lags:])
        row = jnp.concatenate([tail, loads_ref[pl.ds(k, 1), :lags]], axis=1)
        hh_ref[at, :], hl_ref[at, :] = split(toeplitz(row, lags)[:, lags:])
    estimate = dot3(mh_ref[...], ml_ref[...], hh_ref[...], hl_ref[...], NN)
    fh_ref[...], fl_ref[...] = split(counts_ref[:, :lags] / estimate)
    away = blocks(sizes, 1 - (me_ref[0] & 1))[0]
    count = away.size
    ones = jnp.ones((ONES, lags), BF16)
    xh = jnp.concatenate([fh_ref[away, :], ones], axis=0)
    xl = jnp.concatenate([fl_ref[away, :], jnp.zeros_like(ones)], axis=0)
    for k in range(0, motif_count, 2):
        at = pl.ds(k * lags, 2 * lags)
        numer = dot3(xh, xl, hh_ref[at, :], hl_ref[at, :], NT)
        for j in range(2):
            there, here = pl.ds((k + j) * lags, lags), slice(j * lags, (j + 1) * lags)
            send_ref[pl.ds(k + j, count, stride=motif_count), :] = numer[:count, here] + numer_ref[away, there]
            denom = numer[count:count + 1, here] + numer_ref[pl.ds(rows, 1), there]
            send_ref[pl.ds(count * motif_count + k + j, 1), :] = denom
            denom_ref[pl.ds(k + j, 1), :] = denom


def away_kernel(sizes, me_ref, fh_ref, fl_ref, hh_ref, hl_ref, numer_ref, *send_refs):
    lags = send_refs[0].shape[1]
    motif_count = hh_ref.shape[0] // lags
    for ref, at in zip(send_refs, blocks(sizes, 1 - (me_ref[0] & 1))[1:]):
        for k in range(0, motif_count, 2):
            both = pl.ds(k * lags, 2 * lags)
            numer = dot3(fh_ref[at, :], fl_ref[at, :], hh_ref[both, :], hl_ref[both, :], NT) + numer_ref[at, both]
            for j in range(2):
                ref[pl.ds(k + j, at.size, stride=motif_count), :] = numer[:, j * lags:(j + 1) * lags]


def home_kernel(sizes, me_ref, fh_ref, fl_ref, hh_ref, hl_ref, denom_ref, numer_ref, *keep_refs):
    rows, lags = fh_ref.shape
    motif_count = denom_ref.shape[0]
    home = blocks(sizes, me_ref[0] & 1)
    xh = jnp.concatenate([fh_ref[at, :] for at in home], axis=0)
    xl = jnp.concatenate([fl_ref[at, :] for at in home], axis=0)
    for k in range(0, motif_count, 2):
        at = pl.ds(k * lags, 2 * lags)
        numer = dot3(xh, xl, hh_ref[at, :], hl_ref[at, :], NT)
        for j in range(2):
            there, here = pl.ds((k + j) * lags, lags), slice(j * lags, (j + 1) * lags)
            for ref, at, slab in zip(keep_refs, home, slabs(numer, sizes)):
                ref[pl.ds(k + j, at.size, stride=motif_count), :] = slab[:, here] + numer_ref[at, there]
    keep_refs[0][pl.ds(home[0].size * motif_count, motif_count), :] = denom_ref[...]


def fold_kernel(step, steps, half, me_ref, mine_ref, got_ref, send_ref, keep_ref):
    bit = place(me_ref[0], step, steps)
    for out, part in ((send_ref, 1 - bit), (keep_ref, bit)):
        at = pl.ds(part * half, half)
        out[:half] = mine_ref[at] + got_ref[at]
        if out.shape[0] > half:
            out[half:] = mine_ref[2 * half:] + got_ref[2 * half:]


def pair_kernel(me_ref, mine_ref, got_ref, out_ref):
    out_ref[...] = mine_ref[...] + got_ref[...]


def pair_row_kernel(me_ref, mine_ref, got_ref, row_ref, out_ref):
    rows = mine_ref.shape[0]
    out_ref[:rows] = mine_ref[...] + got_ref[...]
    out_ref[rows] = row_ref[...]


def carry(me, bit, mine, got):
    return jnp.where(me & ((1 << bit) - 1) == 0, got, mine)


def carry_bit(me, step, steps):
    first, second = (order(core, steps)[step] for core in range(2))
    return jnp.where(me & 1 == 0, first, second)


def update_kernel(first, size, steps, me_ref, mine_ref, got_ref, denom_ref, motifs_ref, out_ref, *denom_out):
    rows, at, me = size >> (steps - 1), first, me_ref[0]
    for step in range(steps - 1):
        size //= 2
        at = at + place(me, step, steps) * size
    numer = mine_ref[:rows] + got_ref[:rows]
    if denom_out:
        denom = mine_ref[rows] + got_ref[rows]
        denom_out[0][...] = denom
    else:
        denom = denom_ref[...]
    at_row = mine_ref.shape[0] - 1
    row = carry(me, steps - 1, mine_ref[at_row], got_ref[at_row])
    for i in range(rows, out_ref.shape[0]):
        out_ref[i] = row
    out_ref[:rows] = motifs_ref[pl.ds(at, rows)] * numer / denom[None]


def join_kernel(step, steps, size, half, me_ref, mine_ref, got_ref, out_ref):
    me = me_ref[0]
    bit = place(me, step, steps)
    for i in range(half // size):
        here = pl.ds(i * size, size)
        out_ref[pl.ds(2 * i * size + bit * size, size)] = mine_ref[here]
        out_ref[pl.ds(2 * i * size + (1 - bit) * size, size)] = got_ref[here]
    span = 1 << carry_bit(me, step, steps)
    row = jnp.where((me & (span - 1)) == span - 2, got_ref[half], mine_ref[half])
    for i in range(2 * half, out_ref.shape[0]):
        out_ref[i] = row


def store_kernel(parts, row_at, ranks, me_ref, *refs):
    refs, sems = refs[:-1], refs[-1]
    core = me_ref[0] & 1
    copies = []
    out_hbm = refs[-1] if row_at is None else refs[-3]
    for i, ((at, rows, own), block) in enumerate(zip(parts, refs)):
        at = at + (core if own else 1 - core) * rows
        copies.append(pltpu.make_async_copy(block.at[pl.ds(0, rows)], out_hbm.at[pl.ds(at, rows)], sems.at[i]))
    for copy in copies:
        copy.start()
    if row_at is not None:
        block, (numer_ref, scale_ref) = refs[0], refs[len(parts):len(parts) + 2]
        loads_hbm, loads_ref = refs[-2:]
        frames, lags = numer_ref.shape[1], block.shape[-1]
        rest = frames - lags
        ahead = jnp.where(me_ref[0] == ranks - 1, 0.0, block[row_at])
        loads_ref[:, :rest] = scale_ref[:, :rest] * numer_ref[:, :rest]
        loads_ref[:, rest:] = scale_ref[:, rest:] * (numer_ref[:, rest:] + ahead)
        copies.append(pltpu.make_async_copy(loads_ref, loads_hbm, sems.at[len(parts)]))
        copies[-1].start()
    for copy in copies:
        copy.wait()


def lagged_kernel(me_ref, mh_ref, ml_ref, fh_ref, fl_ref, rh_ref, rl_ref, total_ref, out_ref, ph, pw):
    motif_count, lags = total_ref.shape
    frames = out_ref.shape[1] - 2 * lags
    width = frames + lags
    down = lax.broadcasted_iota(jnp.int32, (lags, lags), 0)
    across = lax.broadcasted_iota(jnp.int32, (lags, lags), 1)
    flip = (down + across == lags - 1).astype(BF16)
    xh = jnp.concatenate([fh_ref[...], rh_ref[...]], axis=1)
    xl = jnp.concatenate([fl_ref[...], rl_ref[...]], axis=1)
    for k in range(motif_count):
        at = pl.ds(k * lags, lags)
        for ref, out in ((mh_ref, ph), (ml_ref, pw)):
            out[:, at] = lax.dot_general(ref[:, at], flip, NN, preferred_element_type=F32).astype(BF16)
    for k in range(0, motif_count, 4):
        at = pl.ds(k * lags, 4 * lags)
        lagged = dot3(ph[:, at], pw[:, at], xh, xl, TN)
        for j in range(4):
            wide = jnp.concatenate([jnp.zeros((lags, lags), F32), lagged[j * lags:(j + 1) * lags]], axis=1)
            skewed = pltpu.roll(wide, width - (lags - 1), 1, stride=1, stride_axis=0)
            numer = jnp.sum(skewed, axis=0, keepdims=True)
            out_ref[pl.ds(k + j, 1), :frames] = numer[:, lags:]
            out_ref[pl.ds(k + j, 1), frames:width] = numer[:, :lags]
    out_ref[:, width:] = total_ref[...]


def loads_kernel(ranks, me_ref, mine_ref, got_ref, loads_ref, ahead_ref, numer_ref, scale_ref):
    frames, lags = loads_ref.shape[1], ahead_ref.shape[1]
    both = mine_ref[...] + got_ref[...]
    numer_ref[...] = both[:, :frames]
    ahead_ref[...] = both[:, frames:frames + lags]
    left = (ranks - me_ref[0]) * frames
    lag = lax.broadcasted_iota(jnp.int32, (lags, frames), 0)
    frame = lax.broadcasted_iota(jnp.int32, (lags, frames), 1)
    valid = (lag + frame < left).astype(F32)
    total = both[:, frames + lags:]
    denom = lax.dot_general(total, valid, NN, precision=lax.Precision.HIGHEST, preferred_element_type=F32)
    scale_ref[...] = loads_ref[...] / denom


def body(counts, motifs, loadings):
    rows, motif_count, lags = motifs.shape
    frames = loadings.shape[1]
    ranks, groups = lax.axis_size("tm"), lax.axis_size("neur")
    steps, flips = ranks.bit_length() - 1, groups.bit_length() - 1
    assert ranks == 1 << steps and groups == 1 << flips and steps >= 3

    def shape(*dims, dtype=F32):
        return jax.ShapeDtypeStruct(dims, dtype)

    def swap(x, step):
        return lax.ppermute(x, "tm", [(i, i ^ (1 << order(i & 1, steps)[step])) for i in range(ranks)])

    call = Chain(lax.axis_index("tm").astype(jnp.int32).reshape(1))
    flat = motifs.reshape(rows * motif_count, lags)
    depth, rest = motif_count * lags, frames - lags
    macs = rows * depth * frames * 3
    (call.token,) = call(open_kernel, [shape(motif_count, lags)], flops=10 ** 10)
    call.token, sent = lax.optimization_barrier((call.token, loadings))
    tail = lax.ppermute(sent, "tm", [(i, (i + 1) % ranks) for i in range(ranks)])
    mh, ml, rh, rl, numer, total = call(
        body_kernel,
        [shape(rows, depth, dtype=BF16)] * 2 + [shape(rows, rest, dtype=BF16)] * 2
        + [shape(rows + ONES, depth), shape(motif_count, lags)],
        counts, flat, loadings, scratch=[pltpu.VMEM((depth, rest), BF16)] * 2, limit=BODY_LIMIT, flops=4 * macs,
    )
    head_counts, own_loads = counts, loadings
    sizes = [rows * share // sum(PARTS) for share in PARTS]
    assert sum(sizes) == rows and all(size % (ranks // 2) == 0 for size in sizes)
    chunks = range(len(sizes))
    half = [size // 2 for size in sizes]
    extra = [int(c == 0) for c in chunks]
    parts = [shape((half[c] + extra[c]) * motif_count, lags) for c in chunks]
    send, fh, fl, hh, hl, denom = call(
        functools.partial(head_kernel, sizes),
        parts[:1] + [shape(rows, lags, dtype=BF16)] * 2 + [shape(depth, lags, dtype=BF16)] * 2 + [shape(motif_count, lags)],
        tail, head_counts, own_loads, mh, ml, numer, limit=6,
    )


    def cube(x):
        return x.reshape(-1, motif_count, lags)

    def cubes(count):
        return shape(count, motif_count, lags)

    later = call(functools.partial(away_kernel, sizes), parts[1:], fh, fl, hh, hl, numer, limit=6)
    send = [send, *later]
    got = [swap(cube(x), 0) for x in send]
    keep = call(
        functools.partial(home_kernel, sizes), parts, fh, fl, hh, hl, denom, numer, limit=6, flops=macs // 4
    )
    keep = [cube(x) for x in keep]
    for step in range(1, steps - 1):
        for c in chunks:
            half[c] //= 2
            send[c], keep[c] = call(
                functools.partial(fold_kernel, step, steps, half[c]), [cubes(half[c] + extra[c])] * 2, keep[c], got[c]
            )
            got[c] = swap(send[c], step)
        if step == 1:
            (part,) = call(
                lagged_kernel, [shape(motif_count, frames + 2 * lags)], mh, ml, fh, fl, rh, rl, total,
                scratch=[pltpu.VMEM((rows, depth), BF16)] * 2, limit=8, flops=2 * macs,
            )
            other = jnp.zeros_like(part)
            for flip in range(flips):
                if flip:
                    (part,) = call(pair_kernel, [part], part, other, order=False)
                other = lax.ppermute(part, "neur", [(i, i ^ (1 << flip)) for i in range(groups)])
    last = chunks[-1]
    for c in chunks:
        if c == last:
            ahead, numer, scale = call(
                functools.partial(loads_kernel, ranks), [shape(motif_count, lags)] + [shape(motif_count, frames)] * 2,
                part, other, own_loads,
            )
            (keep[c],) = call(pair_row_kernel, [cubes(half[c] + extra[c] + 1)], keep[c], got[c], ahead)
        else:
            (keep[c],) = call(pair_row_kernel, [cubes(half[c] + extra[c] + 1)], keep[c], got[c], denom)
        got[c] = swap(keep[c], steps - 1)
    carried = [1 + (c != last) for c in chunks]
    mine = [None for c in chunks]
    for c in chunks:
        mine[c], *more = call(
            functools.partial(update_kernel, sum(sizes[:c]), sizes[c], steps),
            [cubes(half[c] + carried[c])] + [shape(motif_count, lags)] * extra[c], keep[c], got[c], denom, motifs,
        )
        if more:
            denom = more[0]
        got[c] = swap(mine[c], 1)
    out, new_loadings, waiting = None, None, []
    size = list(half)
    for step in range(1, steps - 1):
        for c in chunks:
            (mine[c],) = call(
                functools.partial(join_kernel, step, steps, size[c], half[c]), [cubes(2 * half[c] + carried[c])], mine[c], got[c]
            )
            half[c] *= 2
            got[c] = swap(mine[c], (step + 1) % (steps - 1))
            if step == steps - 2:
                waiting.append((sum(sizes[:c]), half[c], True, mine[c]))
                out, new_loadings = store(call, out, new_loadings, rows, waiting, numer, scale, ranks)
                waiting = [(sum(sizes[:c]), half[c], False, got[c])]
    out, new_loadings = store(call, out, new_loadings, rows, waiting, numer, scale, ranks)
    return out, new_loadings


def store(call, out, new_loadings, rows, waiting, numer, scale, ranks):
    waiting = sorted(waiting, key=lambda block: block[2])
    first, half, own, block = waiting[0]
    brings = len(waiting) == 1 and not own
    given = [block for *_, block in waiting] + [numer, scale] * brings
    spaces = [pltpu.VMEM] * len(given)
    results = [jax.ShapeDtypeStruct((rows, *block.shape[1:]), F32)] + [jax.ShapeDtypeStruct(numer.shape, F32)] * brings
    aliases = {}
    if out is not None:
        given.append(out)
        spaces.append(pltpu.HBM)
        aliases = {len(given): 0}
    out, *more = call(
        functools.partial(store_kernel, [place[:3] for place in waiting], half if brings else None, ranks),
        results, *given, spaces=spaces, outs=[pltpu.HBM] * len(results), aliases=aliases,
        scratch=[pltpu.VMEM(numer.shape, F32)] * brings + [pltpu.SemaphoreType.DMA((3,))],
    )
    return out, more[0] if brings else new_loadings


def solution(mesh):
    in_specs = (P("neur", "tm"), P("neur", None, None), P(None, "tm"))
    out_specs = (P("neur", None, None), P(None, "tm"))
    return jax.shard_map(body, mesh=mesh, in_specs=in_specs, out_specs=out_specs, check_vma=False)
```

```python
import functools
import math

import jax
import jax.numpy as jnp
from jax import lax
from jax.experimental import pallas as pl
from jax.experimental.pallas import tpu as pltpu
from jax.sharding import PartitionSpec as P

F32, BF16 = jnp.float32, jnp.bfloat16
NN = (((1,), (0,)), ((), ()))
NT = (((1,), (1,)), ((), ()))
TN = (((0,), (0,)), ((), ()))
MIB = 1024 * 1024
BODY_LIMIT = 20
ONES = 16
PARTS = (1, 1)


def split(x):
    high = x.astype(BF16)
    return high, (x - high.astype(F32)).astype(BF16)


def dot3(ah, al, bh, bl, dims):
    def dot(a, b):
        return lax.dot_general(a, b, dims, preferred_element_type=F32)

    return dot(ah, bh) + (dot(ah, bl) + dot(al, bh))


def toeplitz(row, lags):
    return pltpu.roll(jnp.broadcast_to(row, (lags, row.shape[1])), 0, 1, stride=1, stride_axis=0)


def place(me, step, steps):
    first, second = (order(core, steps)[step] for core in range(2))
    return jnp.where(me & 1 == 0, (me >> first) & 1, (me >> second) & 1)


def order(core, steps):
    return [0, *range(3, steps), 1, 2] if core else list(range(steps))


class Chain:
    def __init__(self, me):
        self.me, self.token = me, None

    def __call__(self, kernel, out_shapes, *args, limit=4, spaces=None, outs=None, scratch=(), aliases=None, flops=0,
                 order=True):
        spaces = spaces or [pltpu.VMEM] * len(args)
        outs = outs or [pltpu.VMEM] * len(out_shapes)
        aliases, tokens = dict(aliases or {}), []
        if order and self.token is not None:
            tokens = [self.token]
            aliases[len(args) + 1] = len(out_shapes)
        given, results = 1 + len(args), len(out_shapes)

        def run(*refs):
            inputs, rest = refs[:given], refs[given + len(tokens):]
            kernel(*inputs, *rest[:results], *rest[results + len(tokens):])

        made = pl.pallas_call(
            run,
            out_shape=[*out_shapes, *(jax.ShapeDtypeStruct(t.shape, t.dtype) for t in tokens)],
            in_specs=[pl.BlockSpec(memory_space=space) for space in [pltpu.SMEM, *spaces, *[pltpu.VMEM] * len(tokens)]],
            out_specs=[pl.BlockSpec(memory_space=space) for space in [*outs, *[pltpu.VMEM] * len(tokens)]],
            scratch_shapes=list(scratch),
            input_output_aliases=aliases,
            compiler_params=pltpu.CompilerParams(vmem_limit_bytes=int(limit * MIB)),
            cost_estimate=pl.CostEstimate(flops=flops, bytes_accessed=0, transcendentals=0),
            name=getattr(kernel, "func", kernel).__name__,
        )(self.me, *args, *tokens)
        if tokens:
            self.token = made[-1]
        return made[:results]


def open_kernel(me_ref, out_ref):
    out_ref[...] = jnp.zeros_like(out_ref)


def body_kernel(me_ref, counts_ref, motifs_ref, loads_ref, mh_ref, ml_ref, rh_ref, rl_ref, numer_ref, th, tl):
    rows, frames = counts_ref.shape
    motif_count, lags = loads_ref.shape[0], motifs_ref.shape[1]
    for k in range(motif_count):
        at = pl.ds(k * lags, lags)
        th[at, :], tl[at, :] = split(toeplitz(loads_ref[pl.ds(k, 1), :], lags)[:, lags:])
        mh_ref[:, at], ml_ref[:, at] = split(motifs_ref[pl.ds(k, rows, stride=motif_count), :])
    estimate = dot3(mh_ref[...], ml_ref[...], th[...], tl[...], NN)
    rh_ref[...], rl_ref[...] = split(counts_ref[:, lags:] / estimate)
    ones = jnp.ones((ONES, frames - lags), BF16)
    xh = jnp.concatenate([rh_ref[...], ones], axis=0)
    xl = jnp.concatenate([rl_ref[...], jnp.zeros_like(ones)], axis=0)
    for k in range(0, motif_count, 2):
        at = pl.ds(k * lags, 2 * lags)
        numer_ref[:, at] = dot3(xh, xl, th[at, :], tl[at, :], NT)


def blocks(sizes, core):
    at = [sum(sizes[:c]) for c in range(len(sizes))]
    step = math.gcd(*sizes) // 2
    return [pl.ds(pl.multiple_of(first + core * (size // 2), step), size // 2) for first, size in zip(at, sizes)]


def slabs(numer, sizes):
    return [numer[sum(sizes[:c]) // 2:sum(sizes[:c + 1]) // 2] for c in range(len(sizes))]


def head_kernel(sizes, me_ref, tail_ref, counts_ref, loads_ref, mh_ref, ml_ref, numer_ref, *refs):
    send_ref, fh_ref, fl_ref, hh_ref, hl_ref, denom_ref = refs
    rows, frames = counts_ref.shape
    motif_count, lags = denom_ref.shape
    for k in range(motif_count):
        at = pl.ds(k * lags, lags)
        tail = jnp.where(me_ref[0] == 0, 0.0, tail_ref[pl.ds(k, 1), frames - lags:])
        row = jnp.concatenate([tail, loads_ref[pl.ds(k, 1), :lags]], axis=1)
        hh_ref[at, :], hl_ref[at, :] = split(toeplitz(row, lags)[:, lags:])
    estimate = dot3(mh_ref[...], ml_ref[...], hh_ref[...], hl_ref[...], NN)
    fh_ref[...], fl_ref[...] = split(counts_ref[:, :lags] / estimate)
    away = blocks(sizes, 1 - (me_ref[0] & 1))[0]
    count = away.size
    ones = jnp.ones((ONES, lags), BF16)
    xh = jnp.concatenate([fh_ref[away, :], ones], axis=0)
    xl = jnp.concatenate([fl_ref[away, :], jnp.zeros_like(ones)], axis=0)
    for k in range(0, motif_count, 2):
        at = pl.ds(k * lags, 2 * lags)
        numer = dot3(xh, xl, hh_ref[at, :], hl_ref[at, :], NT)
        for j in range(2):
            there, here = pl.ds((k + j) * lags, lags), slice(j * lags, (j + 1) * lags)
            send_ref[pl.ds(k + j, count, stride=motif_count), :] = numer[:count, here] + numer_ref[away, there]
            denom = numer[count:count + 1, here] + numer_ref[pl.ds(rows, 1), there]
            send_ref[pl.ds(count * motif_count + k + j, 1), :] = denom
            denom_ref[pl.ds(k + j, 1), :] = denom


def away_kernel(sizes, me_ref, fh_ref, fl_ref, hh_ref, hl_ref, numer_ref, *send_refs):
    lags = send_refs[0].shape[1]
    motif_count = hh_ref.shape[0] // lags
    for ref, at in zip(send_refs, blocks(sizes, 1 - (me_ref[0] & 1))[1:]):
        for k in range(0, motif_count, 2):
            both = pl.ds(k * lags, 2 * lags)
            numer = dot3(fh_ref[at, :], fl_ref[at, :], hh_ref[both, :], hl_ref[both, :], NT) + numer_ref[at, both]
            for j in range(2):
                ref[pl.ds(k + j, at.size, stride=motif_count), :] = numer[:, j * lags:(j + 1) * lags]


def home_kernel(sizes, me_ref, fh_ref, fl_ref, hh_ref, hl_ref, denom_ref, numer_ref, *keep_refs):
    rows, lags = fh_ref.shape
    motif_count = denom_ref.shape[0]
    home = blocks(sizes, me_ref[0] & 1)
    xh = jnp.concatenate([fh_ref[at, :] for at in home], axis=0)
    xl = jnp.concatenate([fl_ref[at, :] for at in home], axis=0)
    for k in range(0, motif_count, 2):
        at = pl.ds(k * lags, 2 * lags)
        numer = dot3(xh, xl, hh_ref[at, :], hl_ref[at, :], NT)
        for j in range(2):
            there, here = pl.ds((k + j) * lags, lags), slice(j * lags, (j + 1) * lags)
            for ref, at, slab in zip(keep_refs, home, slabs(numer, sizes)):
                ref[pl.ds(k + j, at.size, stride=motif_count), :] = slab[:, here] + numer_ref[at, there]
    keep_refs[0][pl.ds(home[0].size * motif_count, motif_count), :] = denom_ref[...]


def fold_kernel(step, steps, half, me_ref, mine_ref, got_ref, send_ref, keep_ref):
    bit = place(me_ref[0], step, steps)
    for out, part in ((send_ref, 1 - bit), (keep_ref, bit)):
        at = pl.ds(part * half, half)
        out[:half] = mine_ref[at] + got_ref[at]
        if out.shape[0] > half:
            out[half:] = mine_ref[2 * half:] + got_ref[2 * half:]


def pair_kernel(me_ref, mine_ref, got_ref, out_ref):
    out_ref[...] = mine_ref[...] + got_ref[...]


def pair_row_kernel(me_ref, mine_ref, got_ref, row_ref, out_ref):
    rows = mine_ref.shape[0]
    out_ref[:rows] = mine_ref[...] + got_ref[...]
    out_ref[rows] = row_ref[...]


def carry(me, bit, mine, got):
    return jnp.where(me & ((1 << bit) - 1) == 0, got, mine)


def carry_bit(me, step, steps):
    first, second = (order(core, steps)[step] for core in range(2))
    return jnp.where(me & 1 == 0, first, second)


def update_kernel(first, size, steps, me_ref, mine_ref, got_ref, denom_ref, motifs_ref, out_ref, *denom_out):
    rows, at, me = size >> (steps - 1), first, me_ref[0]
    for step in range(steps - 1):
        size //= 2
        at = at + place(me, step, steps) * size
    numer = mine_ref[:rows] + got_ref[:rows]
    if denom_out:
        denom = mine_ref[rows] + got_ref[rows]
        denom_out[0][...] = denom
    else:
        denom = denom_ref[...]
    at_row = mine_ref.shape[0] - 1
    row = carry(me, steps - 1, mine_ref[at_row], got_ref[at_row])
    for i in range(rows, out_ref.shape[0]):
        out_ref[i] = row
    out_ref[:rows] = motifs_ref[pl.ds(at, rows)] * numer / denom[None]


def join_kernel(step, steps, size, half, me_ref, mine_ref, got_ref, out_ref):
    me = me_ref[0]
    bit = place(me, step, steps)
    for i in range(half // size):
        here = pl.ds(i * size, size)
        out_ref[pl.ds(2 * i * size + bit * size, size)] = mine_ref[here]
        out_ref[pl.ds(2 * i * size + (1 - bit) * size, size)] = got_ref[here]
    span = 1 << carry_bit(me, step, steps)
    row = jnp.where((me & (span - 1)) == span - 2, got_ref[half], mine_ref[half])
    for i in range(2 * half, out_ref.shape[0]):
        out_ref[i] = row


def store_kernel(parts, row_at, ranks, me_ref, *refs):
    refs, sems = refs[:-1], refs[-1]
    core = me_ref[0] & 1
    copies = []
    out_hbm = refs[-1] if row_at is None else refs[-3]
    for i, ((at, rows, own), block) in enumerate(zip(parts, refs)):
        at = at + (core if own else 1 - core) * rows
        copies.append(pltpu.make_async_copy(block.at[pl.ds(0, rows)], out_hbm.at[pl.ds(at, rows)], sems.at[i]))
    for copy in copies:
        copy.start()
    if row_at is not None:
        block, (numer_ref, scale_ref) = refs[0], refs[len(parts):len(parts) + 2]
        loads_hbm, loads_ref = refs[-2:]
        frames, lags = numer_ref.shape[1], block.shape[-1]
        rest = frames - lags
        ahead = jnp.where(me_ref[0] == ranks - 1, 0.0, block[row_at])
        loads_ref[:, :rest] = scale_ref[:, :rest] * numer_ref[:, :rest]
        loads_ref[:, rest:] = scale_ref[:, rest:] * (numer_ref[:, rest:] + ahead)
        copies.append(pltpu.make_async_copy(loads_ref, loads_hbm, sems.at[len(parts)]))
        copies[-1].start()
    for copy in copies:
        copy.wait()


def lagged_kernel(me_ref, mh_ref, ml_ref, fh_ref, fl_ref, rh_ref, rl_ref, out_ref, ph, pw):
    motif_count = out_ref.shape[0]
    lags = mh_ref.shape[1] // motif_count
    frames = out_ref.shape[1] - 2 * lags
    width = frames + lags
    down = lax.broadcasted_iota(jnp.int32, (lags, lags), 0)
    across = lax.broadcasted_iota(jnp.int32, (lags, lags), 1)
    flip = (down + across == lags - 1).astype(BF16)
    xh = jnp.concatenate([fh_ref[...], rh_ref[...]], axis=1)
    xl = jnp.concatenate([fl_ref[...], rl_ref[...]], axis=1)
    for k in range(motif_count):
        at = pl.ds(k * lags, lags)
        for ref, out in ((mh_ref, ph), (ml_ref, pw)):
            out[:, at] = lax.dot_general(ref[:, at], flip, NN, preferred_element_type=F32).astype(BF16)
        motifs = mh_ref[:, at].astype(F32) + ml_ref[:, at].astype(F32)
        out_ref[pl.ds(k, 1), width:] = jnp.sum(motifs, axis=0, keepdims=True)
    for k in range(0, motif_count, 4):
        at = pl.ds(k * lags, 4 * lags)
        lagged = dot3(ph[:, at], pw[:, at], xh, xl, TN)
        for j in range(4):
            wide = jnp.concatenate([jnp.zeros((lags, lags), F32), lagged[j * lags:(j + 1) * lags]], axis=1)
            skewed = pltpu.roll(wide, width - (lags - 1), 1, stride=1, stride_axis=0)
            numer = jnp.sum(skewed, axis=0, keepdims=True)
            out_ref[pl.ds(k + j, 1), :frames] = numer[:, lags:]
            out_ref[pl.ds(k + j, 1), frames:width] = numer[:, :lags]


def loads_kernel(ranks, me_ref, mine_ref, got_ref, loads_ref, ahead_ref, numer_ref, scale_ref):
    frames, lags = loads_ref.shape[1], ahead_ref.shape[1]
    both = mine_ref[...] + got_ref[...]
    numer_ref[...] = both[:, :frames]
    ahead_ref[...] = both[:, frames:frames + lags]
    left = (ranks - me_ref[0]) * frames
    lag = lax.broadcasted_iota(jnp.int32, (lags, frames), 0)
    frame = lax.broadcasted_iota(jnp.int32, (lags, frames), 1)
    valid = (lag + frame < left).astype(F32)
    total = both[:, frames + lags:]
    denom = lax.dot_general(total, valid, NN, precision=lax.Precision.HIGHEST, preferred_element_type=F32)
    scale_ref[...] = loads_ref[...] / denom


def body(counts, motifs, loadings):
    rows, motif_count, lags = motifs.shape
    frames = loadings.shape[1]
    ranks, groups = lax.axis_size("tm"), lax.axis_size("neur")
    steps, flips = ranks.bit_length() - 1, groups.bit_length() - 1
    assert ranks == 1 << steps and groups == 1 << flips and steps >= 3

    def shape(*dims, dtype=F32):
        return jax.ShapeDtypeStruct(dims, dtype)

    def swap(x, step):
        return lax.ppermute(x, "tm", [(i, i ^ (1 << order(i & 1, steps)[step])) for i in range(ranks)])

    call = Chain(lax.axis_index("tm").astype(jnp.int32).reshape(1))
    flat = motifs.reshape(rows * motif_count, lags)
    depth, rest = motif_count * lags, frames - lags
    macs = rows * depth * frames * 3
    (call.token,) = call(open_kernel, [shape(motif_count, lags)], flops=10 ** 10)
    call.token, sent = lax.optimization_barrier((call.token, loadings))
    tail = lax.ppermute(sent, "tm", [(i, (i + 1) % ranks) for i in range(ranks)])
    mh, ml, rh, rl, numer = call(
        body_kernel,
        [shape(rows, depth, dtype=BF16)] * 2 + [shape(rows, rest, dtype=BF16)] * 2
        + [shape(rows + ONES, depth)],
        counts, flat, loadings, scratch=[pltpu.VMEM((depth, rest), BF16)] * 2, limit=BODY_LIMIT, flops=4 * macs,
    )
    head_counts, own_loads = counts, loadings
    sizes = [rows * share // sum(PARTS) for share in PARTS]
    assert sum(sizes) == rows and all(size % (ranks // 2) == 0 for size in sizes)
    chunks = range(len(sizes))
    half = [size // 2 for size in sizes]
    extra = [int(c == 0) for c in chunks]
    parts = [shape((half[c] + extra[c]) * motif_count, lags) for c in chunks]
    send, fh, fl, hh, hl, denom = call(
        functools.partial(head_kernel, sizes),
        parts[:1] + [shape(rows, lags, dtype=BF16)] * 2 + [shape(depth, lags, dtype=BF16)] * 2 + [shape(motif_count, lags)],
        tail, head_counts, own_loads, mh, ml, numer, limit=6,
    )


    def cube(x):
        return x.reshape(-1, motif_count, lags)

    def cubes(count):
        return shape(count, motif_count, lags)

    later = call(functools.partial(away_kernel, sizes), parts[1:], fh, fl, hh, hl, numer, limit=6)
    send = [send, *later]
    got = [swap(cube(x), 0) for x in send]
    keep = call(
        functools.partial(home_kernel, sizes), parts, fh, fl, hh, hl, denom, numer, limit=6, flops=macs // 4
    )
    keep = [cube(x) for x in keep]
    for step in range(1, steps - 1):
        for c in chunks:
            half[c] //= 2
            send[c], keep[c] = call(
                functools.partial(fold_kernel, step, steps, half[c]), [cubes(half[c] + extra[c])] * 2, keep[c], got[c]
            )
            got[c] = swap(send[c], step)
        if step == 1:
            (part,) = call(
                lagged_kernel, [shape(motif_count, frames + 2 * lags)], mh, ml, fh, fl, rh, rl,
                scratch=[pltpu.VMEM((rows, depth), BF16)] * 2, limit=8, flops=2 * macs,
            )
            other = jnp.zeros_like(part)
            for flip in range(flips):
                if flip:
                    (part,) = call(pair_kernel, [part], part, other, order=False)
                other = lax.ppermute(part, "neur", [(i, i ^ (1 << flip)) for i in range(groups)])
    last = chunks[-1]
    for c in chunks:
        if c == last:
            ahead, numer, scale = call(
                functools.partial(loads_kernel, ranks), [shape(motif_count, lags)] + [shape(motif_count, frames)] * 2,
                part, other, own_loads,
            )
            (keep[c],) = call(pair_row_kernel, [cubes(half[c] + extra[c] + 1)], keep[c], got[c], ahead)
        else:
            (keep[c],) = call(pair_row_kernel, [cubes(half[c] + extra[c] + 1)], keep[c], got[c], denom)
        got[c] = swap(keep[c], steps - 1)
    carried = [1 + (c != last) for c in chunks]
    mine = [None for c in chunks]
    for c in chunks:
        mine[c], *more = call(
            functools.partial(update_kernel, sum(sizes[:c]), sizes[c], steps),
            [cubes(half[c] + carried[c])] + [shape(motif_count, lags)] * extra[c], keep[c], got[c], denom, motifs,
        )
        if more:
            denom = more[0]
        got[c] = swap(mine[c], 1)
    out, new_loadings, waiting = None, None, []
    size = list(half)
    for step in range(1, steps - 1):
        for c in chunks:
            (mine[c],) = call(
                functools.partial(join_kernel, step, steps, size[c], half[c]), [cubes(2 * half[c] + carried[c])], mine[c], got[c]
            )
            half[c] *= 2
            got[c] = swap(mine[c], (step + 1) % (steps - 1))
            if step == steps - 2:
                waiting.append((sum(sizes[:c]), half[c], True, mine[c]))
                out, new_loadings = store(call, out, new_loadings, rows, waiting, numer, scale, ranks)
                waiting = [(sum(sizes[:c]), half[c], False, got[c])]
    out, new_loadings = store(call, out, new_loadings, rows, waiting, numer, scale, ranks)
    return out, new_loadings


def store(call, out, new_loadings, rows, waiting, numer, scale, ranks):
    waiting = sorted(waiting, key=lambda block: block[2])
    first, half, own, block = waiting[0]
    brings = len(waiting) == 1 and not own
    given = [block for *_, block in waiting] + [numer, scale] * brings
    spaces = [pltpu.VMEM] * len(given)
    results = [jax.ShapeDtypeStruct((rows, *block.shape[1:]), F32)] + [jax.ShapeDtypeStruct(numer.shape, F32)] * brings
    aliases = {}
    if out is not None:
        given.append(out)
        spaces.append(pltpu.HBM)
        aliases = {len(given): 0}
    out, *more = call(
        functools.partial(store_kernel, [place[:3] for place in waiting], half if brings else None, ranks),
        results, *given, spaces=spaces, outs=[pltpu.HBM] * len(results), aliases=aliases,
        scratch=[pltpu.VMEM(numer.shape, F32)] * brings + [pltpu.SemaphoreType.DMA((3,))],
    )
    return out, more[0] if brings else new_loadings


def solution(mesh):
    in_specs = (P("neur", "tm"), P("neur", None, None), P(None, "tm"))
    out_specs = (P("neur", None, None), P(None, "tm"))
    return jax.shard_map(body, mesh=mesh, in_specs=in_specs, out_specs=out_specs, check_vma=False)
```
